256 devices in a mesh: row: 32 (over z, y_hi, core), col: 8 (over x, y_lo).
Axes of the slice: x: 4, y: 4 (y_hi: 2, y_lo: 2; y = y_hi * 2 + y_lo), z: 8, core: 2. Of those that a mesh axis runs over, the one named last changes fastest.
Arguments:
- inputs: bfloat16 [32, 8, 2, 128, 1024], P('row', 'col'), may hold values from -6 to 6
- targets: bfloat16 [32, 8, 2, 128, 1024], P('row', 'col'), may hold values from -6 to 6
- up_master: float32 [8, 1024, 2048], P('col', 'row'), may hold values from -6 to 6
- up_momentum: float32 [8, 1024, 2048], P('col', 'row'), may hold values from -0.75 to 0.75
- down_master: float32 [32, 2048, 1024], P('row', 'col'), may hold values from -6 to 6
- down_momentum: float32 [32, 2048, 1024], P('row', 'col'), may hold values from -0.75 to 0.75
Outputs:
- new_up: float32 [8, 1024, 2048], P('col', 'row')
- new_up_momentum: float32 [8, 1024, 2048], P('col', 'row')
- new_down: float32 [32, 2048, 1024], P('row', 'col')
- new_down_momentum: float32 [32, 2048, 1024], P('row', 'col')
The draws below stay inside these ranges and needn't reach their ends.
All inputs are finite; a program needn't handle non-finite values.
Results may differ from the reference program's by a relative error of at most 0.015.
The reference program's roundings to bfloat16 on the way (of `normed`, `act`, `grad_out` and `grad_pre`) count: a program that leaves them out, or rounds other values in their place, can miss the bound.
Values may be sent and summed in bfloat16 or wider, within the bound.
No kernel may reach another device: no remote copies, remote signals or barrier semaphores. Data moves between devices by JAX's collectives and lax.ppermute only.
A program may use at most 128 MiB of HBM per device.

```python
import jax
import jax.numpy as jnp
from jax import lax

D = 1024
FFW = 2048
TOK = 128
INNER = 2
MOD1 = 8
MOD2 = 32
N_ROW = 32
N_COL = 8


def shard_levels(key, dims, pieces, least, high):
    def one(dim, parts):
        steps = jax.random.uniform(jax.random.fold_in(jax.random.fold_in(key, 6), dim), (parts,), jnp.float32, least / len(pieces), high / len(pieces))
        return jnp.repeat(jnp.exp(steps), dims[dim] // parts).reshape((-1,) + (1,) * (len(dims) - dim - 1))

    loudness = one(*pieces[0])
    for cut in pieces[1:]:
        loudness = loudness * one(*cut)
    return loudness


def gaussian(key, dims, width, limit, pieces=(), kind=jnp.bfloat16):
    array = width * jax.random.normal(key, dims, jnp.float32)
    if pieces:
        array = array * shard_levels(key, dims, pieces, -0.22, 0.18)
    return jnp.clip(array, -limit, limit).astype(kind)


def setup_inputs(seed: int = 0) -> dict:
    arg_keys = jax.random.split(jax.random.key(seed), 7)
    inputs = gaussian(arg_keys[0], (N_ROW, N_COL, INNER, TOK, D), 1.0, 6.0, ((0, 32), (1, 8)))
    targets = gaussian(arg_keys[1], (N_ROW, N_COL, INNER, TOK, D), 1.0, 6.0, ((0, 32), (1, 8)))
    up_master = gaussian(arg_keys[2], (MOD1, D, FFW), 1.0, 6.0, ((0, 8), (1, 32)), jnp.float32)
    up_momentum = gaussian(arg_keys[3], (MOD1, D, FFW), 0.05, 0.75, ((0, 8), (1, 32)), jnp.float32)
    down_master = gaussian(arg_keys[4], (MOD2, FFW, D), 1.0, 6.0, ((0, 32), (1, 8)), jnp.float32)
    down_momentum = gaussian(arg_keys[5], (MOD2, FFW, D), 0.05, 0.75, ((0, 32), (1, 8)), jnp.float32)
    return dict(inputs=inputs, targets=targets, up_master=up_master, up_momentum=up_momentum, down_master=down_master, down_momentum=down_momentum)


adam_rate = 0.05
beta_one = 0.9
beta_two = 0.95
adam_eps = 1e-06
decay_rate = 0.1
outer_rate = 0.7
outer_beta = 0.9
norm_eps = 1e-06

def forward_part(up_used, down_used, batch_in, batch_target):
    width_scale = up_used.shape[0] ** (-0.5)
    hidden_scale = up_used.shape[1] ** (-0.5)
    token_count = batch_in.shape[0]
    feats = batch_in.astype(jnp.float32)
    square_mean = lax.optimization_barrier(jnp.mean(feats * feats, axis=-1, keepdims=True))
    normed = (feats * lax.rsqrt(square_mean + norm_eps)).astype(jnp.bfloat16)
    pre = jnp.dot(normed, up_used, preferred_element_type=jnp.float32) * width_scale
    act = jax.nn.gelu(pre).astype(jnp.bfloat16)
    outval = jnp.dot(act, down_used, preferred_element_type=jnp.float32) * hidden_scale
    resid = feats + outval - batch_target.astype(jnp.float32)
    grad_out = (resid / token_count).astype(jnp.bfloat16)
    return (normed, pre, act, grad_out)

def down_gradient(act, grad_out, hidden_scale):
    return lax.dot_general(act, grad_out, (((0,), (0,)), ((), ())), preferred_element_type=jnp.float32) * hidden_scale

def up_gradient(normed, pre, grad_out, down_used):
    width_scale = normed.shape[1] ** (-0.5)
    hidden_scale = down_used.shape[0] ** (-0.5)
    grad_act = lax.dot_general(grad_out, down_used, (((1,), (1,)), ((), ())), preferred_element_type=jnp.float32) * hidden_scale
    unused, pull = jax.vjp(jax.nn.gelu, pre)
    grad_pre = pull(grad_act)[0].astype(jnp.bfloat16)
    return lax.dot_general(normed, grad_pre, (((0,), (0,)), ((), ())), preferred_element_type=jnp.float32) * width_scale

def adam_update(param, first, second, grad, step_num):
    first = beta_one * first + (1.0 - beta_one) * grad
    second = beta_two * second + (1.0 - beta_two) * grad * grad
    first_hat = first / (1.0 - beta_one ** step_num)
    second_hat = second / (1.0 - beta_two ** step_num)
    param = param - adam_rate * (first_hat / (jnp.sqrt(second_hat) + adam_eps) + decay_rate * param)
    return (param, first, second)

def path_changes(start_up, start_down, path_in, path_target):
    up_param = start_up.astype(jnp.float32)
    down_param = start_down.astype(jnp.float32)
    up_first = jnp.zeros_like(up_param)
    up_second = jnp.zeros_like(up_param)
    down_first = jnp.zeros_like(down_param)
    down_second = jnp.zeros_like(down_param)
    hidden_scale = start_up.shape[1] ** (-0.5)
    for step_idx in range(path_in.shape[0]):
        up_used = up_param.astype(jnp.bfloat16)
        down_used = down_param.astype(jnp.bfloat16)
        normed, pre, act, grad_out = forward_part(up_used, down_used, path_in[step_idx], path_target[step_idx])
        grad_down = down_gradient(act, grad_out, hidden_scale)
        grad_up = up_gradient(normed, pre, grad_out, down_used)
        down_param, down_first, down_second = adam_update(down_param, down_first, down_second, grad_down, step_idx + 1)
        up_param, up_first, up_second = adam_update(up_param, up_first, up_second, grad_up, step_idx + 1)
    up_change = (start_up.astype(jnp.float32) - up_param).astype(jnp.bfloat16)
    down_change = (start_down.astype(jnp.float32) - down_param).astype(jnp.bfloat16)
    return (up_change, down_change)

def reference(inputs, targets, up_master, up_momentum, down_master, down_momentum):

    def visit(carry, path_idx):
        up_sums, down_sums = carry
        row_idx = path_idx // N_COL
        col_idx = path_idx % N_COL
        start_up = lax.dynamic_index_in_dim(up_master, col_idx, 0, keepdims=False).astype(jnp.bfloat16)
        start_down = lax.dynamic_index_in_dim(down_master, row_idx, 0, keepdims=False).astype(jnp.bfloat16)
        row_in = lax.dynamic_index_in_dim(inputs, row_idx, 0, keepdims=False)
        path_in = lax.dynamic_index_in_dim(row_in, col_idx, 0, keepdims=False)
        row_target = lax.dynamic_index_in_dim(targets, row_idx, 0, keepdims=False)
        path_target = lax.dynamic_index_in_dim(row_target, col_idx, 0, keepdims=False)
        up_change, down_change = path_changes(start_up, start_down, path_in, path_target)
        up_change = lax.optimization_barrier(up_change).astype(jnp.float32)
        down_change = lax.optimization_barrier(down_change).astype(jnp.float32)
        up_sums = up_sums.at[col_idx].add(up_change)
        down_sums = down_sums.at[row_idx].add(down_change)
        return ((up_sums, down_sums), None)
    init = (jnp.zeros(up_master.shape, jnp.float32), jnp.zeros(down_master.shape, jnp.float32))
    sums, unused = lax.scan(visit, init, jnp.arange(N_ROW * N_COL, dtype=jnp.int32))
    up_avg = sums[0] / N_ROW
    down_avg = sums[1] / N_COL
    new_up_momentum = outer_beta * up_momentum + up_avg
    new_up = up_master - outer_rate * (up_avg + outer_beta * new_up_momentum)
    new_down_momentum = outer_beta * down_momentum + down_avg
    new_down = down_master - outer_rate * (down_avg + outer_beta * new_down_momentum)
    return (new_up, new_up_momentum, new_down, new_down_momentum)
```

```python
import jax
import jax.numpy as jnp
from jax import lax
from jax.sharding import PartitionSpec as P

adam_rate = 0.05
beta_one = 0.9
beta_two = 0.95
adam_eps = 1e-06
decay_rate = 0.1
outer_rate = 0.7
outer_beta = 0.9
norm_eps = 1e-06

bf16 = jnp.bfloat16
f32 = jnp.float32


def swap_core(a):
    return lax.ppermute(a, "row", [(i, i ^ 1) for i in range(32)])


def swap_yh(a):
    return lax.ppermute(a, "row", [(i, i ^ 2) for i in range(32)])


def from_z(a, k):
    return lax.ppermute(a, "row", [(i, (i - 4 * k) % 32) for i in range(32)])


def swap_yl(a):
    return lax.ppermute(a, "col", [(i, i ^ 1) for i in range(8)])


def from_x(a, k):
    return lax.ppermute(a, "col", [(i, (i - 2 * k) % 8) for i in range(8)])


def gather_up(a):
    b = swap_yh(a)
    own = jnp.concatenate([a, b], 0)
    p1, m1 = from_z(own, 1), from_z(own, -1)
    p2, m2 = from_z(p1, 1), from_z(m1, -1)
    p3, m3 = from_z(p2, 1), from_z(m2, -1)
    p4, m4 = from_z(p3[:32], 1), from_z(m3[32:], -1)
    half = jnp.concatenate([own, p1, p2, p3, p4, m4, m3, m2, m1], 0)
    other = swap_core(half)
    return jnp.concatenate([half, other], 0)


def gather_down(a):
    a1, a3, b0 = from_x(a, 1), from_x(a, -1), swap_yl(a)
    plus = from_x(jnp.concatenate([a1[:128], b0[:128]], 0), 1)
    minus = from_x(jnp.concatenate([a3[128:], b0[128:]], 0), -1)
    cross = swap_yl(jnp.concatenate([a1[128:], a3[:128]], 0))
    a2 = jnp.concatenate([plus[:128], minus[:128]], 0)
    b1 = jnp.concatenate([plus[128:], cross[:128]], 0)
    b3 = jnp.concatenate([cross[128:], minus[128:]], 0)
    b2 = jnp.concatenate([from_x(b1[:80], 1), from_x(b3[80:160], -1), swap_yl(a2[160:])], 0)
    return jnp.concatenate([a, a1, a2, a3, b0, b1, b2, b3], 0)


def add(a, b):
    return (a.astype(f32) + b.astype(f32)).astype(bf16)


def scatter_up(v):
    got = swap_core(v[512:])
    c = [add(v[64 * k : 64 * k + 64], got[64 * k : 64 * k + 64]) for k in range(8)]
    p, m = from_z(c[4][:32], -1), from_z(c[4][32:], 1)
    c3 = jnp.concatenate([add(c[3][:32], p), c[3][32:]], 0)
    c5 = jnp.concatenate([c[5][:32], add(c[5][32:], m)], 0)
    p, m = from_z(c3, -1), from_z(c5, 1)
    c2, c6 = add(c[2], p), add(c[6], m)
    p, m = from_z(c2, -1), from_z(c6, 1)
    c1, c7 = add(c[1], p), add(c[7], m)
    p, m = from_z(c1, -1), from_z(c7, 1)
    c0 = c[0].astype(f32) + p.astype(f32) + m.astype(f32)
    return c0[:32] + swap_yh(c0[32:].astype(bf16)).astype(f32)


def scatter_down(v):
    t0, t1, t2, t3, u0, u1, u2, u3 = [v[256 * k : 256 * k + 256] for k in range(8)]
    p, m, w = from_x(u2[:80], -1), from_x(u2[80:160], 1), swap_yl(u2[160:])
    u1 = jnp.concatenate([add(u1[:80], p), u1[80:]], 0)
    u3 = jnp.concatenate([u3[:80], add(u3[80:160], m), u3[160:]], 0)
    t2 = jnp.concatenate([t2[:160], add(t2[160:], w)], 0)
    p = from_x(jnp.concatenate([t2[:128], u1[:128]], 0), -1)
    m = from_x(jnp.concatenate([t2[128:], u3[128:]], 0), 1)
    w = swap_yl(jnp.concatenate([u1[128:], u3[:128]], 0))
    t1 = jnp.concatenate([add(t1[:128], p[:128]), add(t1[128:], w[:128])], 0)
    t3 = jnp.concatenate([add(t3[:128], w[128:]), add(t3[128:], m[:128])], 0)
    u0 = jnp.concatenate([add(u0[:128], p[128:]), add(u0[128:], m[128:])], 0)
    p, m, w = from_x(t1, -1), from_x(t3, 1), swap_yl(u0)
    return t0.astype(f32) + p.astype(f32) + m.astype(f32) + w.astype(f32)


def block_order():
    col = lax.axis_index("col")
    x, yl = col // 2, col % 2
    place = [((x + k % 4) % 4) * 2 + (yl + k // 4) % 2 for k in range(8)]
    slot = [((b % 2 + yl) % 2) * 4 + (b // 2 - x + 4) % 4 for b in range(8)]
    return place, slot


def pick(a, order):
    return jnp.concatenate(
        [lax.dynamic_slice_in_dim(a, 256 * k, 256, 1) for k in order], 1
    )


def feature_order():
    row = lax.axis_index("row")
    z, yh, core = row // 4, (row // 2) % 2, row % 2
    rel = lax.broadcasted_iota(jnp.int32, (1, 1024), 1)
    dc, dz, dyh, lane = rel // 512, (rel // 64) % 8, (rel // 32) % 2, rel % 32
    place = (((z + dz) % 8) * 4 + ((yh + dyh) % 2) * 2 + (core + dc) % 2) * 32 + lane
    return (lax.broadcasted_iota(jnp.int32, (1024, 1024), 0) == place).astype(bf16)


def local(inputs, targets, up_master, up_momentum, down_master, down_momentum):
    start_up = gather_up(up_master[0].astype(bf16))
    start_down = gather_down(down_master[0].astype(bf16))
    width_scale = 1024 ** (-0.5)
    hidden_scale = 2048 ** (-0.5)
    feats = inputs[0, 0].astype(f32)
    square_mean = jnp.mean(feats * feats, axis=-1, keepdims=True)
    normed = (feats * lax.rsqrt(square_mean + norm_eps)).astype(bf16)
    normed = jnp.einsum("tnd,de->tne", normed, feature_order(), preferred_element_type=f32).astype(bf16)
    resid_part = feats - targets[0, 0].astype(f32)
    place, slot = block_order()

    def dot(a, b, dims):
        return lax.dot_general(a, b, (dims, ((), ())), preferred_element_type=f32)

    def step(up_used, down_used, t):
        pre = dot(normed[t], up_used, ((1,), (0,))) * width_scale
        act = pick(jax.nn.gelu(pre).astype(bf16), place)
        outval = dot(act, down_used, ((1,), (0,))) * hidden_scale
        grad_out = ((resid_part[t] + outval) / 128).astype(bf16)
        grad_act = pick(dot(grad_out, down_used, ((1,), (1,))) * hidden_scale, slot)
        unused, pull = jax.vjp(jax.nn.gelu, pre)
        grad_pre = pull(grad_act)[0].astype(bf16)
        grad_down = dot(act, grad_out, ((0,), (0,))) * hidden_scale
        grad_up = dot(normed[t], grad_pre, ((0,), (0,))) * width_scale
        return grad_up, grad_down

    def first(start, grad):
        return start - adam_rate * (grad / (jnp.abs(grad) + adam_eps) + decay_rate * start)

    def second(param, grad_one, grad_two):
        one = (beta_one * (1 - beta_one)) * grad_one + (1 - beta_one) * grad_two
        two = (beta_two * (1 - beta_two)) * grad_one * grad_one + (1 - beta_two) * grad_two * grad_two
        one = one / (1 - beta_one**2)
        two = two / (1 - beta_two**2)
        return param - adam_rate * (one / (jnp.sqrt(two) + adam_eps) + decay_rate * param)

    up_start, down_start = start_up.astype(f32), start_down.astype(f32)
    up_one, down_one = step(start_up, start_down, 0)
    up_param, down_param = first(up_start, up_one), first(down_start, down_one)
    up_two, down_two = step(up_param.astype(bf16), down_param.astype(bf16), 1)
    down_change = (down_start - second(down_param, down_one, down_two)).astype(bf16)
    up_change = (up_start - second(up_param, up_one, up_two)).astype(bf16)
    down_avg = scatter_down(down_change) / 8
    up_avg = scatter_up(up_change) / 32
    new_up_momentum = outer_beta * up_momentum + up_avg[None]
    new_up = up_master - outer_rate * (up_avg[None] + outer_beta * new_up_momentum)
    new_down_momentum = outer_beta * down_momentum + down_avg[None]
    new_down = down_master - outer_rate * (down_avg[None] + outer_beta * new_down_momentum)
    return (new_up, new_up_momentum, new_down, new_down_momentum)


def solution(mesh):
    in_specs = (
        P("row", "col", None, None, None),
        P("row", "col", None, None, None),
        P("col", "row", None),
        P("col", "row", None),
        P("row", "col", None),
        P("row", "col", None),
    )
    out_specs = (
        P("col", "row", None),
        P("col", "row", None),
        P("row", "col", None),
        P("row", "col", None),
    )
    return jax.shard_map(local, mesh=mesh, in_specs=in_specs, out_specs=out_specs, check_vma=False)
```

```python
import jax
import jax.numpy as jnp
from jax import lax
from jax.experimental import pallas as pl
from jax.experimental.pallas import tpu as pltpu
from jax.sharding import PartitionSpec as P

adam_rate = 0.05
beta_one = 0.9
beta_two = 0.95
adam_eps = 1e-06
decay_rate = 0.1
outer_rate = 0.7
outer_beta = 0.9
norm_eps = 1e-06

bf16 = jnp.bfloat16
f32 = jnp.float32

TOK, D, FFW = 128, 1024, 2048
BLK = 256
SEND, KEEP = 448, 576
width_scale = D ** (-0.5)
hidden_scale = FFW ** (-0.5)
ROOT = (2 / 3.141592653589793) ** 0.5


def swap_core(a):
    return lax.ppermute(a, "row", [(i, i ^ 1) for i in range(32)])


def swap_yh(a):
    return lax.ppermute(a, "row", [(i, i ^ 2) for i in range(32)])


def from_z(a):
    return lax.ppermute(a, "row", [(i, (i + (4 if i % 2 else -4)) % 32) for i in range(32)])


def to_z(a):
    return lax.ppermute(a, "row", [(i, (i + (-4 if i % 2 else 4)) % 32) for i in range(32)])


def swap_yl(a):
    return lax.ppermute(a, "col", [(i, i ^ 1) for i in range(8)])


def from_x(a, k):
    return lax.ppermute(a, "col", [(i, (i - 2 * k) % 8) for i in range(8)])


def up_order():
    side = [(k, y, c) for y in range(2) for k in (1, 2, 3) for c in range(2)]
    side += [(4, 0, 0), (4, 1, 0)]
    other = [(-k, y, 1 - c) for k, y, c in side]
    own = [(0, 0, 0), (0, 1, 0), (0, 0, 1), (0, 1, 1)]
    return other, side, own


def gather_up(a):
    b = swap_yh(a)
    aa, bb = swap_core(a), swap_core(b)
    own = [a, b, aa, bb]
    side, four = [], []
    for x, xx in ((a, aa), (b, bb)):
        now = jnp.concatenate([x, xx], 0)
        for k in range(3):
            now = from_z(now)
            side.append(now)
        four.append(from_z(now[:32]))
    side = side + four
    return [swap_core(s) for s in side], side, own


def gather_down(a):
    a1, a3, b0 = from_x(a, 1), from_x(a, -1), swap_yl(a)
    plus = from_x(jnp.concatenate([a1[:128], b0[:128]], 0), 1)
    minus = from_x(jnp.concatenate([a3[128:], b0[128:]], 0), -1)
    cross = swap_yl(jnp.concatenate([a1[128:], a3[:128]], 0))
    last_p, last_m = from_x(plus[128:208], 1), from_x(minus[176:], -1)
    last_y = swap_yl(jnp.concatenate([plus[80:128], minus[:48]], 0))
    return [
        (a, 0, 256, 0),
        (a1, 0, 256, 256),
        (plus, 0, 128, 512),
        (minus, 0, 128, 640),
        (a3, 0, 256, 768),
        (b0, 0, 256, 1024),
        (plus, 128, 128, 1280),
        (cross, 0, 128, 1408),
        (last_p, 0, 80, 1536),
        (last_y, 0, 96, 1616),
        (last_m, 0, 80, 1712),
        (cross, 128, 128, 1792),
        (minus, 128, 128, 1920),
    ]


def add(a, b):
    return (a.astype(f32) + b.astype(f32)).astype(bf16)


def scatter_up(other, keep):
    got = swap_core(other)
    rest = []
    for y in range(2):
        at = 192 * y
        c = [add(keep[at + 64 * k : at + 64 * k + 64], got[at + 64 * k : at + 64 * k + 64]) for k in range(3)]
        p = to_z(add(keep[384 + 32 * y : 416 + 32 * y], got[384 + 32 * y : 416 + 32 * y]))
        p = to_z(jnp.concatenate([add(c[2][:32], p), c[2][32:]], 0))
        p = to_z(add(c[1], p))
        rest.append(to_z(add(c[0], p)))
    a, b = rest
    own = keep[SEND:].astype(f32)
    mine = own[:64] + jnp.concatenate([a[:32], b[:32]], 0).astype(f32)
    away = own[64:] + jnp.concatenate([a[32:], b[32:]], 0).astype(f32)
    mine = mine + swap_core(away.astype(bf16)).astype(f32)
    return mine[:32] + swap_yh(mine[32:].astype(bf16)).astype(f32)


def scatter_down(v):
    t0, t1, t2, t3, u0, u1, u2, u3 = [v[256 * k : 256 * k + 256] for k in range(8)]
    p, m, w = from_x(u2[:80], -1), from_x(u2[176:], 1), swap_yl(u2[80:176])
    p = from_x(jnp.concatenate([t2[:80], add(t2[80:128], w[:48]), add(u1[:80], p), u1[80:128]], 0), -1)
    m = from_x(jnp.concatenate([add(t2[128:176], w[48:]), t2[176:], u3[128:176], add(u3[176:], m)], 0), 1)
    w = swap_yl(jnp.concatenate([u1[128:], u3[:128]], 0))
    t1 = jnp.concatenate([add(t1[:128], p[:128]), add(t1[128:], w[:128])], 0)
    t3 = jnp.concatenate([add(t3[:128], w[128:]), add(t3[128:], m[:128])], 0)
    u0 = jnp.concatenate([add(u0[:128], p[128:]), add(u0[128:], m[128:])], 0)
    p, m, w = from_x(t1, -1), from_x(t3, 1), swap_yl(u0)
    return t0.astype(f32) + p.astype(f32) + m.astype(f32) + w.astype(f32)


def hidden_place():
    col = lax.axis_index("col")
    x, yl = col // 2, col % 2
    return jnp.stack([((x + k % 4) % 4) * 2 + (yl + k // 4) % 2 for k in range(8)]).astype(jnp.int32)


def feature_order():
    row = lax.axis_index("row")
    z, yh, core = row // 4, (row // 2) % 2, row % 2
    sign = 1 - 2 * core
    other, side, own = up_order()
    first = jnp.stack(
        [((z + sign * k) % 8) * 4 + ((yh + y) % 2) * 2 + (core + c) % 2 for k, y, c in other + side + own]
    )
    place = (first[:, None] * 32 + jnp.arange(32)[None]).reshape(1, D)
    return (lax.broadcasted_iota(jnp.int32, (D, D), 0) == place).astype(bf16)


def dot(a, b, dims=((1,), (0,))):
    return lax.dot_general(a, b, (dims, ((), ())), preferred_element_type=f32)


def gelu(x):
    return 0.5 * x * (1.0 + jnp.tanh(ROOT * (x + 0.044715 * x * x * x)))


def gelu_slope(x):
    t = jnp.tanh(ROOT * (x + 0.044715 * x * x * x))
    return 0.5 * (1.0 + t) + 0.5 * x * (1.0 - t * t) * (ROOT * (1.0 + 3 * 0.044715 * x * x))


def first_weight(start, raw, scale):
    part = raw / (jnp.abs(raw) + adam_eps / scale)
    return (1 - adam_rate * decay_rate) * start.astype(f32) - adam_rate * part


def change_of(start, one, two, scale):
    eps = adam_eps / scale
    left = 1 - adam_rate * decay_rate
    part_one = one / (jnp.abs(one) + eps)
    ca, cb = (1 - beta_one) * beta_one / (1 - beta_one**2), (1 - beta_one) / (1 - beta_one**2)
    cc, cd = (1 - beta_two) * beta_two / (1 - beta_two**2), (1 - beta_two) / (1 - beta_two**2)
    size = jnp.sqrt(cc * one * one + cd * two * two)
    part_two = (ca * one + cb * two) / (size + eps)
    return (
        (adam_rate * left) * part_one
        + adam_rate * part_two
        + (1 - left * left) * start.astype(f32)
    ).astype(bf16)


def inner_kernel(up_pieces, down_pieces, *refs):
    count = len(up_pieces) + len(down_pieces)
    place_ref, n_ref, nt_ref, x_ref, t_ref = refs[:5]
    pieces = refs[5 : 5 + count]
    act_ref, g_ref, gp_ref, send_ref, keep_ref, sd_out = refs[5 + count : 11 + count]
    su, sd, w1u, w1d, pre_ref, sem, out_sem = refs[11 + count :]

    up_copies, down_copies = [], []
    for i, (start, rows, at) in enumerate(up_pieces):
        up_copies.append(
            pltpu.make_async_copy(pieces[i].at[pl.ds(start, rows)], su.at[pl.ds(at, rows)], sem.at[i])
        )
    for j, (start, rows, at) in enumerate(down_pieces):
        i = j + len(up_pieces)
        down_copies.append(
            pltpu.make_async_copy(pieces[i].at[pl.ds(start, rows)], sd.at[pl.ds(at, rows)], sem.at[i])
        )
    for c in up_copies + down_copies:
        c.start()
    for c in up_copies:
        c.wait()

    def columns(k):
        return pl.ds(pl.multiple_of(place_ref[k] * BLK, BLK), BLK)

    def slot(k):
        return pl.ds(pl.multiple_of(k * BLK, BLK), BLK)

    @pl.loop(0, 8)
    def _(k):
        pre = dot(n_ref[0], su[:, columns(k)]) * width_scale
        pre_ref[:, slot(k)] = pre
        act_ref[0, :, slot(k)] = gelu(pre).astype(bf16)

    for c in down_copies:
        c.wait()
    outs = [
        pltpu.make_async_copy(su.at[pl.ds(0, SEND)], send_ref, out_sem.at[0]),
        pltpu.make_async_copy(su.at[pl.ds(SEND, KEEP)], keep_ref, out_sem.at[1]),
        pltpu.make_async_copy(sd, sd_out, out_sem.at[2]),
    ]
    for c in outs:
        c.start()

    def grad_out(t, weight):
        @pl.loop(0, D // BLK)
        def _(j):
            outval = dot(act_ref[t], weight[:, slot(j)]) * hidden_scale
            resid = x_ref[t, :, slot(j)].astype(f32) + outval - t_ref[t, :, slot(j)].astype(f32)
            g_ref[t, :, slot(j)] = (resid * (1.0 / TOK)).astype(bf16)

    def grad_pre(t, weight):
        @pl.loop(0, 8)
        def _(k):
            grad_act = dot(g_ref[t], weight[slot(k), :], ((1,), (1,))) * hidden_scale
            gp_ref[t, :, columns(k)] = (grad_act * gelu_slope(pre_ref[:, slot(k)])).astype(bf16)

    grad_out(0, sd)
    grad_pre(0, sd)

    @pl.loop(0, 8)
    def _(k):
        raw = dot(nt_ref[...], gp_ref[0, :, columns(k)])
        w1u[...] = first_weight(su[:, columns(k)], raw, width_scale).astype(bf16)
        raw = dot(act_ref[0, :, slot(k)], g_ref[0], ((0,), (0,)))
        w1d[slot(k), :] = first_weight(sd[slot(k), :], raw, hidden_scale).astype(bf16)
        pre = dot(n_ref[1], w1u[...]) * width_scale
        pre_ref[:, slot(k)] = pre
        act_ref[1, :, slot(k)] = gelu(pre).astype(bf16)

    grad_out(1, w1d)
    grad_pre(1, w1d)
    for c in outs:
        c.wait()


def inner_steps(place, normed, normed_t, x, t, up_pieces, down_pieces):
    vmem, hbm = pl.BlockSpec(memory_space=pltpu.VMEM), pl.BlockSpec(memory_space=pl.ANY)
    pieces = [p[0] for p in up_pieces + down_pieces]

    def kernel(*refs):
        inner_kernel([p[1:] for p in up_pieces], [p[1:] for p in down_pieces], *refs)

    return pl.pallas_call(
        kernel,
        out_shape=(
            jax.ShapeDtypeStruct((2, TOK, FFW), bf16),
            jax.ShapeDtypeStruct((2, TOK, D), bf16),
            jax.ShapeDtypeStruct((2, TOK, FFW), bf16),
            jax.ShapeDtypeStruct((SEND, FFW), bf16),
            jax.ShapeDtypeStruct((KEEP, FFW), bf16),
            jax.ShapeDtypeStruct((FFW, D), bf16),
        ),
        in_specs=[pl.BlockSpec(memory_space=pltpu.SMEM)] + [vmem] * 4 + [hbm] * len(pieces),
        out_specs=(vmem, vmem, vmem, hbm, hbm, hbm),
        scratch_shapes=[
            pltpu.VMEM((D, FFW), bf16),
            pltpu.VMEM((FFW, D), bf16),
            pltpu.VMEM((D, BLK), bf16),
            pltpu.VMEM((FFW, D), bf16),
            pltpu.VMEM((TOK, FFW), f32),
            pltpu.SemaphoreType.DMA((len(pieces),)),
            pltpu.SemaphoreType.DMA((3,)),
        ],
        compiler_params=pltpu.CompilerParams(vmem_limit_bytes=36 * 1024 * 1024),
        cost_estimate=pl.CostEstimate(flops=5 * 10**9, bytes_accessed=24 * 2**20, transcendentals=0),
        name="inner_steps",
    )(place, normed, normed_t, x, t, *pieces)


def up_change(start, normed_t, grad_pre):
    rows = start.shape[0]

    def kernel(s_ref, n_ref, g_ref, o_ref):
        one = dot(n_ref[0], g_ref[0])
        two = dot(n_ref[1], g_ref[1])
        o_ref[...] = change_of(s_ref[...], one, two, width_scale)

    return pl.pallas_call(
        kernel,
        grid=(FFW // BLK,),
        out_shape=jax.ShapeDtypeStruct((rows, FFW), bf16),
        in_specs=[
            pl.BlockSpec((rows, BLK), lambda j: (0, j)),
            pl.BlockSpec((2, rows, TOK), lambda j: (0, 0, 0)),
            pl.BlockSpec((2, TOK, BLK), lambda j: (0, 0, j)),
        ],
        out_specs=pl.BlockSpec((rows, BLK), lambda j: (0, j)),
        compiler_params=pltpu.CompilerParams(vmem_limit_bytes=24 * 1024 * 1024),
        cost_estimate=pl.CostEstimate(flops=4 * rows * TOK * FFW, bytes_accessed=4 * rows * FFW, transcendentals=0),
        name="up_change",
    )(start, normed_t, grad_pre)


def down_change(start, act, grad_out):
    def kernel(s_ref, a_ref, g_ref, o_ref):
        one = dot(a_ref[0], g_ref[0], ((0,), (0,)))
        two = dot(a_ref[1], g_ref[1], ((0,), (0,)))
        o_ref[...] = change_of(s_ref[...], one, two, hidden_scale)

    return pl.pallas_call(
        kernel,
        grid=(FFW // BLK,),
        out_shape=jax.ShapeDtypeStruct((FFW, D), bf16),
        in_specs=[
            pl.BlockSpec((BLK, D), lambda k: (k, 0)),
            pl.BlockSpec((2, TOK, BLK), lambda k: (0, 0, k)),
            pl.BlockSpec((2, TOK, D), lambda k: (0, 0, 0)),
        ],
        out_specs=pl.BlockSpec((BLK, D), lambda k: (k, 0)),
        compiler_params=pltpu.CompilerParams(vmem_limit_bytes=24 * 1024 * 1024),
        cost_estimate=pl.CostEstimate(flops=4 * FFW * TOK * D, bytes_accessed=4 * FFW * D, transcendentals=0),
        name="down_change",
    )(start, act, grad_out)


def local(inputs, targets, up_master, up_momentum, down_master, down_momentum):
    other, side, own = gather_up(up_master[0].astype(bf16))
    down_pieces = gather_down(down_master[0].astype(bf16))
    up_pieces, at = [], 0
    for a in other + side + own:
        up_pieces.append((a, 0, a.shape[0], at))
        at += a.shape[0]

    x, t = inputs[0, 0], targets[0, 0]
    feats = x.astype(f32)
    square_mean = jnp.mean(feats * feats, axis=-1, keepdims=True)
    normed = (feats * lax.rsqrt(square_mean + norm_eps)).astype(bf16)
    order = feature_order()
    rel = jnp.einsum("tnd,de->tne", normed, order, preferred_element_type=f32).astype(bf16)
    rel_t = jnp.swapaxes(rel, 1, 2)

    act, grad_out, grad_pre, up_other, up_keep, down_start = inner_steps(
        hidden_place(), rel, rel_t[0], x, t, up_pieces, down_pieces
    )
    down_avg = scatter_down(down_change(down_start, act, grad_out)) / 8
    v_other = up_change(up_other, rel_t[:, :SEND], grad_pre)
    v_keep = up_change(up_keep, rel_t[:, SEND:], grad_pre)
    up_avg = scatter_up(v_other, v_keep) / 32
    new_up_momentum = outer_beta * up_momentum + up_avg[None]
    new_up = up_master - outer_rate * (up_avg[None] + outer_beta * new_up_momentum)
    new_down_momentum = outer_beta * down_momentum + down_avg[None]
    new_down = down_master - outer_rate * (down_avg[None] + outer_beta * new_down_momentum)
    return (new_up, new_up_momentum, new_down, new_down_momentum)


def solution(mesh):
    in_specs = (
        P("row", "col", None, None, None),
        P("row", "col", None, None, None),
        P("col", "row", None),
        P("col", "row", None),
        P("row", "col", None),
        P("row", "col", None),
    )
    out_specs = (
        P("col", "row", None),
        P("col", "row", None),
        P("row", "col", None),
        P("row", "col", None),
    )
    return jax.shard_map(local, mesh=mesh, in_specs=in_specs, out_specs=out_specs, check_vma=False)
```

```python
import jax
import jax.numpy as jnp
from jax import lax
from jax.experimental import pallas as pl
from jax.experimental.pallas import tpu as pltpu
from jax.sharding import PartitionSpec as P

adam_rate = 0.05
beta_one = 0.9
beta_two = 0.95
adam_eps = 1e-06
decay_rate = 0.1
outer_rate = 0.7
outer_beta = 0.9
norm_eps = 1e-06

bf16 = jnp.bfloat16
f32 = jnp.float32

TOK, D, FFW = 128, 1024, 2048
BLK = 256
SEND, KEEP = 448, 576
width_scale = D ** (-0.5)
hidden_scale = FFW ** (-0.5)
ROOT = (2 / 3.141592653589793) ** 0.5


def swap_core(a):
    return lax.ppermute(a, "row", [(i, i ^ 1) for i in range(32)])


def swap_yh(a):
    return lax.ppermute(a, "row", [(i, i ^ 2) for i in range(32)])


def from_z(a, way):
    return lax.ppermute(a, "row", [(i, (i + (4 if (i + way) % 2 else -4)) % 32) for i in range(32)])


def to_z(a, way):
    return from_z(a, 1 - way)


def swap_yl(a):
    return lax.ppermute(a, "col", [(i, i ^ 1) for i in range(8)])


def from_x(a, k):
    return lax.ppermute(a, "col", [(i, (i - 2 * k) % 8) for i in range(8)])


def up_order():
    side = [(k - 2 * k * y, y, c) for y in range(2) for k in (1, 2, 3) for c in range(2)]
    side += [(4, 0, 0), (4, 1, 0)]
    other = [(-k, y, 1 - c) for k, y, c in side]
    own = [(0, 0, 0), (0, 1, 0), (0, 0, 1), (0, 1, 1)]
    return other, side, own


def gather_up(a):
    b = swap_yh(a)
    aa, bb = swap_core(a), swap_core(b)
    own = [a, b, aa, bb]
    side, four = [], []
    for way, (x, xx) in enumerate(((a, aa), (b, bb))):
        now = jnp.concatenate([x, xx], 0)
        for k in range(3):
            now = from_z(now, way)
            side.append(now)
        four.append(from_z(now[:32], way))
    side = side + four
    return [swap_core(s) for s in side], side, own


def gather_down(a):
    a1, a3, b0 = from_x(a, 1), from_x(a, -1), swap_yl(a)
    plus = from_x(jnp.concatenate([a1[:128], b0[:128]], 0), 1)
    minus = from_x(jnp.concatenate([a3[128:], b0[128:]], 0), -1)
    cross = swap_yl(jnp.concatenate([a1[128:], a3[:128]], 0))
    last_p, last_m = from_x(plus[128:208], 1), from_x(minus[176:], -1)
    last_y = swap_yl(jnp.concatenate([plus[80:128], minus[:48]], 0))
    return [
        (a, 0, 256, 0),
        (a1, 0, 256, 256),
        (plus, 0, 128, 512),
        (minus, 0, 128, 640),
        (a3, 0, 256, 768),
        (b0, 0, 256, 1024),
        (plus, 128, 128, 1280),
        (cross, 0, 128, 1408),
        (last_p, 0, 80, 1536),
        (last_y, 0, 96, 1616),
        (last_m, 0, 80, 1712),
        (cross, 128, 128, 1792),
        (minus, 128, 128, 1920),
    ]


def add(a, b):
    return (a.astype(f32) + b.astype(f32)).astype(bf16)


def scatter_up(other, keep):
    got = swap_core(other)
    rest = []
    for y in range(2):
        at = 192 * y
        c = [add(keep[at + 64 * k : at + 64 * k + 64], got[at + 64 * k : at + 64 * k + 64]) for k in range(3)]
        p = to_z(add(keep[384 + 32 * y : 416 + 32 * y], got[384 + 32 * y : 416 + 32 * y]), y)
        p = to_z(jnp.concatenate([add(c[2][:32], p), c[2][32:]], 0), y)
        p = to_z(add(c[1], p), y)
        rest.append(to_z(add(c[0], p), y))
    a, b = rest
    own = keep[SEND:].astype(f32)
    mine = own[:64] + jnp.concatenate([a[:32], b[:32]], 0).astype(f32)
    away = own[64:] + jnp.concatenate([a[32:], b[32:]], 0).astype(f32)
    mine = mine + swap_core(away.astype(bf16)).astype(f32)
    return mine[:32] + swap_yh(mine[32:].astype(bf16)).astype(f32)


def scatter_down(v):
    t0, t1, t2, t3, u0, u1, u2, u3 = [v[256 * k : 256 * k + 256] for k in range(8)]
    p, m, w = from_x(u2[:80], -1), from_x(u2[176:], 1), swap_yl(u2[80:176])
    p = from_x(jnp.concatenate([t2[:80], add(t2[80:128], w[:48]), add(u1[:80], p), u1[80:128]], 0), -1)
    m = from_x(jnp.concatenate([add(t2[128:176], w[48:]), t2[176:], u3[128:176], add(u3[176:], m)], 0), 1)
    w = swap_yl(jnp.concatenate([u1[128:], u3[:128]], 0))
    t1 = jnp.concatenate([add(t1[:128], p[:128]), add(t1[128:], w[:128])], 0)
    t3 = jnp.concatenate([add(t3[:128], w[128:]), add(t3[128:], m[:128])], 0)
    u0 = jnp.concatenate([add(u0[:128], p[128:]), add(u0[128:], m[128:])], 0)
    p, m, w = from_x(t1, -1), from_x(t3, 1), swap_yl(u0)
    return t0.astype(f32) + p.astype(f32) + m.astype(f32) + w.astype(f32)


def hidden_place():
    col = lax.axis_index("col")
    x, yl = col // 2, col % 2
    return jnp.stack([((x + k % 4) % 4) * 2 + (yl + k // 4) % 2 for k in range(8)]).astype(jnp.int32)


def feature_order():
    row = lax.axis_index("row")
    z, yh, core = row // 4, (row // 2) % 2, row % 2
    sign = 1 - 2 * core
    other, side, own = up_order()
    first = jnp.stack(
        [((z + sign * k) % 8) * 4 + ((yh + y) % 2) * 2 + (core + c) % 2 for k, y, c in other + side + own]
    )
    place = (first[:, None] * 32 + jnp.arange(32)[None]).reshape(1, D)
    return (lax.broadcasted_iota(jnp.int32, (D, D), 0) == place).astype(bf16)


def dot(a, b, dims=((1,), (0,))):
    return lax.dot_general(a, b, (dims, ((), ())), preferred_element_type=f32)


def gelu(x):
    return 0.5 * x * (1.0 + jnp.tanh(ROOT * (x + 0.044715 * x * x * x)))


def gelu_slope(x):
    t = jnp.tanh(ROOT * (x + 0.044715 * x * x * x))
    return 0.5 * (1.0 + t) + 0.5 * x * (1.0 - t * t) * (ROOT * (1.0 + 3 * 0.044715 * x * x))


def first_weight(start, raw, scale):
    part = raw / (jnp.abs(raw) + adam_eps / scale)
    return (1 - adam_rate * decay_rate) * start.astype(f32) - adam_rate * part


def change_of(start, one, two, scale):
    eps = adam_eps / scale
    left = 1 - adam_rate * decay_rate
    ca, cb = (1 - beta_one) * beta_one / (1 - beta_one**2), (1 - beta_one) / (1 - beta_one**2)
    cc, cd = (1 - beta_two) * beta_two / (1 - beta_two**2), (1 - beta_two) / (1 - beta_two**2)
    part_one = one / ((jnp.abs(one) + eps) * (1 / (adam_rate * left)))
    square = one * one + (cd / cc) * (two * two)
    size = square * lax.rsqrt(jnp.maximum(square, 1e-36))
    root = cc**0.5
    part_two = (one + (cb / ca) * two) / ((size + eps / root) * (root / (adam_rate * ca)))
    return (part_one + part_two + (1 - left * left) * start.astype(f32)).astype(bf16)


def inner_kernel(up_pieces, down_pieces, *refs):
    count = len(up_pieces) + len(down_pieces)
    place_ref, nt_ref, x_ref, t_ref = refs[:4]
    pieces = refs[4 : 4 + count]
    act_ref, g_ref, gp_ref, send_ref, keep_ref, sd_out = refs[4 + count : 10 + count]
    su, sd, w1u, w1d, pre_ref, n_ref, sem, out_sem = refs[10 + count :]

    up_copies, down_copies = [], []
    for i, (start, rows, at) in enumerate(up_pieces):
        up_copies.append(
            pltpu.make_async_copy(pieces[i].at[pl.ds(start, rows)], su.at[pl.ds(at, rows)], sem.at[i])
        )
    for j, (start, rows, at) in enumerate(down_pieces):
        i = j + len(up_pieces)
        down_copies.append(
            pltpu.make_async_copy(pieces[i].at[pl.ds(start, rows)], sd.at[pl.ds(at, rows)], sem.at[i])
        )
    for c in up_copies + down_copies:
        c.start()
    for t in range(2):
        n_ref[t] = nt_ref[t].T
    for c in up_copies:
        c.wait()

    def columns(k):
        return pl.ds(pl.multiple_of(place_ref[k] * BLK, BLK), BLK)

    def slot(k):
        return pl.ds(pl.multiple_of(k * BLK, BLK), BLK)

    @pl.loop(0, 8)
    def _(k):
        pre = dot(n_ref[0], su[:, columns(k)]) * width_scale
        pre_ref[:, slot(k)] = pre
        act_ref[0, :, slot(k)] = gelu(pre).astype(bf16)

    for c in down_copies:
        c.wait()
    outs = [
        pltpu.make_async_copy(su.at[pl.ds(0, SEND)], send_ref, out_sem.at[0]),
        pltpu.make_async_copy(su.at[pl.ds(SEND, KEEP)], keep_ref, out_sem.at[1]),
        pltpu.make_async_copy(sd, sd_out, out_sem.at[2]),
    ]
    for c in outs:
        c.start()

    def grad_out(t, weight):
        @pl.loop(0, D // BLK)
        def _(j):
            outval = dot(act_ref[t], weight[:, slot(j)]) * hidden_scale
            resid = x_ref[t, :, slot(j)].astype(f32) + outval - t_ref[t, :, slot(j)].astype(f32)
            g_ref[t, :, slot(j)] = (resid * (1.0 / TOK)).astype(bf16)

    def grad_pre(t, weight):
        @pl.loop(0, 8)
        def _(k):
            grad_act = dot(g_ref[t], weight[slot(k), :], ((1,), (1,))) * hidden_scale
            gp_ref[t, :, columns(k)] = (grad_act * gelu_slope(pre_ref[:, slot(k)])).astype(bf16)

    grad_out(0, sd)
    grad_pre(0, sd)

    @pl.loop(0, 8)
    def _(k):
        raw = dot(nt_ref[0], gp_ref[0, :, columns(k)])
        w1u[...] = first_weight(su[:, columns(k)], raw, width_scale).astype(bf16)
        raw = dot(act_ref[0, :, slot(k)], g_ref[0], ((0,), (0,)))
        w1d[slot(k), :] = first_weight(sd[slot(k), :], raw, hidden_scale).astype(bf16)
        pre = dot(n_ref[1], w1u[...]) * width_scale
        pre_ref[:, slot(k)] = pre
        act_ref[1, :, slot(k)] = gelu(pre).astype(bf16)

    grad_out(1, w1d)
    grad_pre(1, w1d)
    for c in outs:
        c.wait()


def inner_steps(place, normed_t, x, t, up_pieces, down_pieces):
    vmem, hbm = pl.BlockSpec(memory_space=pltpu.VMEM), pl.BlockSpec(memory_space=pl.ANY)
    far = pl.BlockSpec(memory_space=pltpu.HBM)
    pieces = [p[0] for p in up_pieces + down_pieces]

    def kernel(*refs):
        inner_kernel([p[1:] for p in up_pieces], [p[1:] for p in down_pieces], *refs)

    return pl.pallas_call(
        kernel,
        out_shape=(
            jax.ShapeDtypeStruct((2, TOK, FFW), bf16),
            jax.ShapeDtypeStruct((2, TOK, D), bf16),
            jax.ShapeDtypeStruct((2, TOK, FFW), bf16),
            jax.ShapeDtypeStruct((SEND, FFW), bf16),
            jax.ShapeDtypeStruct((KEEP, FFW), bf16),
            jax.ShapeDtypeStruct((FFW, D), bf16),
        ),
        in_specs=[pl.BlockSpec(memory_space=pltpu.SMEM)] + [vmem] * 3 + [far] * len(pieces),
        out_specs=(vmem, vmem, vmem, hbm, hbm, hbm),
        scratch_shapes=[
            pltpu.VMEM((D, FFW), bf16),
            pltpu.VMEM((FFW, D), bf16),
            pltpu.VMEM((D, BLK), bf16),
            pltpu.VMEM((FFW, D), bf16),
            pltpu.VMEM((TOK, FFW), f32),
            pltpu.VMEM((2, TOK, D), bf16),
            pltpu.SemaphoreType.DMA((len(pieces),)),
            pltpu.SemaphoreType.DMA((3,)),
        ],
        compiler_params=pltpu.CompilerParams(vmem_limit_bytes=36 * 1024 * 1024),
        cost_estimate=pl.CostEstimate(flops=5 * 10**9, bytes_accessed=24 * 2**20, transcendentals=0),
        name="inner_steps",
    )(place, normed_t, x, t, *pieces)


def up_change(start, normed_t, grad_pre, first):
    rows = start.shape[0]
    wide = 2 * BLK

    def kernel(s_ref, n_ref, g_ref, o_ref):
        one = dot(n_ref[0, pl.ds(first, rows)], g_ref[0])
        two = dot(n_ref[1, pl.ds(first, rows)], g_ref[1])
        o_ref[...] = change_of(s_ref[...], one, two, width_scale)

    return pl.pallas_call(
        kernel,
        grid=(FFW // wide,),
        out_shape=jax.ShapeDtypeStruct((rows, FFW), bf16),
        in_specs=[
            pl.BlockSpec((rows, wide), lambda j: (0, j)),
            pl.BlockSpec((2, D, TOK), lambda j: (0, 0, 0)),
            pl.BlockSpec((2, TOK, wide), lambda j: (0, 0, j)),
        ],
        out_specs=pl.BlockSpec((rows, wide), lambda j: (0, j)),
        compiler_params=pltpu.CompilerParams(vmem_limit_bytes=24 * 1024 * 1024),
        cost_estimate=pl.CostEstimate(flops=4 * rows * TOK * FFW, bytes_accessed=4 * rows * FFW, transcendentals=0),
        name="up_change",
    )(start, normed_t, grad_pre)


def down_change(start, act, grad_out):
    def kernel(s_ref, a_ref, g_ref, o_ref):
        one = dot(a_ref[0], g_ref[0], ((0,), (0,)))
        two = dot(a_ref[1], g_ref[1], ((0,), (0,)))
        o_ref[...] = change_of(s_ref[...], one, two, hidden_scale)

    return pl.pallas_call(
        kernel,
        grid=(FFW // BLK,),
        out_shape=jax.ShapeDtypeStruct((FFW, D), bf16),
        in_specs=[
            pl.BlockSpec((BLK, D), lambda k: (k, 0)),
            pl.BlockSpec((2, TOK, BLK), lambda k: (0, 0, k)),
            pl.BlockSpec((2, TOK, D), lambda k: (0, 0, 0)),
        ],
        out_specs=pl.BlockSpec((BLK, D), lambda k: (k, 0)),
        compiler_params=pltpu.CompilerParams(vmem_limit_bytes=24 * 1024 * 1024),
        cost_estimate=pl.CostEstimate(flops=4 * FFW * TOK * D, bytes_accessed=4 * FFW * D, transcendentals=0),
        name="down_change",
    )(start, act, grad_out)


def local(inputs, targets, up_master, up_momentum, down_master, down_momentum):
    other, side, own = gather_up(up_master[0].astype(bf16))
    down_pieces = gather_down(down_master[0].astype(bf16))
    up_pieces, at = [], 0
    for a in other + side + own:
        up_pieces.append((a, 0, a.shape[0], at))
        at += a.shape[0]

    x, t = inputs[0, 0], targets[0, 0]
    feats = x.astype(f32)
    square_mean = jnp.mean(feats * feats, axis=-1, keepdims=True)
    normed = (feats * lax.rsqrt(square_mean + norm_eps)).astype(bf16)
    order = feature_order()
    rel_t = jnp.einsum("de,tnd->ten", order, normed, preferred_element_type=f32).astype(bf16)

    act, grad_out, grad_pre, up_other, up_keep, down_start = inner_steps(
        hidden_place(), rel_t, x, t, up_pieces, down_pieces
    )
    down_avg = scatter_down(down_change(down_start, act, grad_out)) / 8
    v_other = up_change(up_other, rel_t, grad_pre, 0)
    v_keep = up_change(up_keep, rel_t, grad_pre, SEND)
    up_avg = scatter_up(v_other, v_keep) / 32
    new_up_momentum = outer_beta * up_momentum + up_avg[None]
    new_up = up_master - outer_rate * (up_avg[None] + outer_beta * new_up_momentum)
    new_down_momentum = outer_beta * down_momentum + down_avg[None]
    new_down = down_master - outer_rate * (down_avg[None] + outer_beta * new_down_momentum)
    return (new_up, new_up_momentum, new_down, new_down_momentum)


def solution(mesh):
    in_specs = (
        P("row", "col", None, None, None),
        P("row", "col", None, None, None),
        P("col", "row", None),
        P("col", "row", None),
        P("row", "col", None),
        P("row", "col", None),
    )
    out_specs = (
        P("col", "row", None),
        P("col", "row", None),
        P("row", "col", None),
        P("row", "col", None),
    )
    return jax.shard_map(local, mesh=mesh, in_specs=in_specs, out_specs=out_specs, check_vma=False)
```

```python
import jax
import jax.numpy as jnp
from jax import lax
from jax.experimental import pallas as pl
from jax.experimental.pallas import tpu as pltpu
from jax.sharding import PartitionSpec as P

adam_rate = 0.05
beta_one = 0.9
beta_two = 0.95
adam_eps = 1e-06
decay_rate = 0.1
outer_rate = 0.7
outer_beta = 0.9
norm_eps = 1e-06

bf16 = jnp.bfloat16
f32 = jnp.float32

TOK, D, FFW = 128, 1024, 2048
BLK = 256
SEND, KEEP = 448, 576
EARLY, LATE = 768, 1280
width_scale = D ** (-0.5)
hidden_scale = FFW ** (-0.5)
ROOT = (2 / 3.141592653589793) ** 0.5


def swap_core(a):
    return lax.ppermute(a, "row", [(i, i ^ 1) for i in range(32)])


def swap_yh(a):
    return lax.ppermute(a, "row", [(i, i ^ 2) for i in range(32)])


def from_z(a):
    return lax.ppermute(a, "row", [(i, (i + (4 if i % 2 else -4)) % 32) for i in range(32)])


def to_z(a):
    return lax.ppermute(a, "row", [(i, (i + (-4 if i % 2 else 4)) % 32) for i in range(32)])


def swap_yl(a):
    return lax.ppermute(a, "col", [(i, i ^ 1) for i in range(8)])


def from_x(a, k):
    return lax.ppermute(a, "col", [(i, (i - 2 * k) % 8) for i in range(8)])


def up_order():
    own = [(0, 0, 0), (0, 1, 0), (0, 0, 1), (0, 1, 1)]
    side = [(k, y, c) for k in (1, 2, 3) for _, y, c in own] + [(4, 0, 0), (4, 1, 0)]
    other = [(-k, y, 1 - c) for k, y, c in side]
    return other, side, own


DOWN_ORDER = ((1, 1), (2, 1), (3, 1), (0, 1), (0, 0), (1, 0), (2, 0), (3, 0))


def gather_up(a):
    b = swap_yh(a)
    own = [a, b, swap_core(a), swap_core(b)]
    now, side = jnp.concatenate(own, 0), []
    for k in range(3):
        now = from_z(now)
        side.append(now)
    side.append(from_z(now[:64]))
    return [swap_core(s) for s in side], side, own


def gather_down(a):
    b0 = swap_yl(a)
    a1, a3, a2 = from_x(a, 1), from_x(a, -1), from_x(a, 2)
    return [from_x(b0, 1), swap_yl(a2), from_x(b0, -1), b0, a, a1, a2, a3]


def add(*parts):
    total = parts[0].astype(f32)
    for p in parts[1:]:
        total = total + p.astype(f32)
    return total


def scatter_up(other, keep):
    got = swap_core(other)
    p = to_z(add(keep[384:448], got[384:448]).astype(bf16))
    p = jnp.pad(p, ((0, 64), (0, 0)))
    for at in (256, 128, 0):
        p = to_z(add(keep[at : at + 128], got[at : at + 128], p).astype(bf16))
    away = add(keep[SEND + 64 :], p[64:]).astype(bf16)
    mine = add(keep[SEND : SEND + 64], p[:64], swap_core(away))
    return mine[:32] + swap_yh(mine[32:].astype(bf16)).astype(f32)


def scatter_down(u1, u2, u3, u0, t0, t1, t2, t3):
    p, m, w = from_x(u1, -1), from_x(u3, 1), swap_yl(u2)
    u0 = add(u0, p, m).astype(bf16)
    t2 = add(t2, w).astype(bf16)
    return add(t0, from_x(t1, -1), from_x(t3, 1), from_x(t2, -2), swap_yl(u0))


def hidden_place():
    col = lax.axis_index("col")
    x, yl = col // 2, col % 2
    return jnp.stack([((x + dx) % 4) * 2 + (yl + dyl) % 2 for dx, dyl in DOWN_ORDER]).astype(jnp.int32)


def feature_order():
    row = lax.axis_index("row")
    z, yh, core = row // 4, (row // 2) % 2, row % 2
    sign = 1 - 2 * core
    other, side, own = up_order()
    first = jnp.stack(
        [((z + sign * k) % 8) * 4 + ((yh + y) % 2) * 2 + (core + c) % 2 for k, y, c in other + side + own]
    )
    place = (first[:, None] * 32 + jnp.arange(32)[None]).reshape(1, D)
    return (lax.broadcasted_iota(jnp.int32, (D, D), 0) == place).astype(bf16)


def dot(a, b, dims=((1,), (0,))):
    return lax.dot_general(a, b, (dims, ((), ())), preferred_element_type=f32)


def gelu(x):
    return 0.5 * x * (1.0 + jnp.tanh(ROOT * (x + 0.044715 * x * x * x)))


def gelu_slope(x):
    t = jnp.tanh(ROOT * (x + 0.044715 * x * x * x))
    return 0.5 * (1.0 + t) + 0.5 * x * (1.0 - t * t) * (ROOT * (1.0 + 3 * 0.044715 * x * x))


def first_weight(start, raw, scale):
    part = raw / (jnp.abs(raw) + adam_eps / scale)
    return (1 - adam_rate * decay_rate) * start.astype(f32) - adam_rate * part


def change_of(start, one, two, scale):
    eps = adam_eps / scale
    left = 1 - adam_rate * decay_rate
    ca, cb = (1 - beta_one) * beta_one / (1 - beta_one**2), (1 - beta_one) / (1 - beta_one**2)
    cc, cd = (1 - beta_two) * beta_two / (1 - beta_two**2), (1 - beta_two) / (1 - beta_two**2)
    part_one = one / ((jnp.abs(one) + eps) * (1 / (adam_rate * left)))
    square = one * one + (cd / cc) * (two * two)
    size = square * lax.rsqrt(jnp.maximum(square, 1e-36))
    root = cc**0.5
    part_two = (one + (cb / ca) * two) / ((size + eps / root) * (root / (adam_rate * ca)))
    return (part_one + part_two + (1 - left * left) * start.astype(f32)).astype(bf16)


def inner_kernel(up_pieces, down_pieces, *refs):
    count = len(up_pieces) + len(down_pieces)
    place_ref, nt_ref, x_ref, t_ref = refs[:4]
    pieces = refs[4 : 4 + count]
    act_ref, g_ref, gp_ref, send_ref, keep_ref, early_ref, late_ref = refs[4 + count : 11 + count]
    su, sd, w1u, w1d, pre_ref, n_ref, sem, out_sem = refs[11 + count :]

    up_copies, down_copies = [], []
    for i, (start, rows, at) in enumerate(up_pieces):
        up_copies.append(
            pltpu.make_async_copy(pieces[i].at[pl.ds(start, rows)], su.at[pl.ds(at, rows)], sem.at[i])
        )
    for j, (start, rows, at) in enumerate(down_pieces):
        i = j + len(up_pieces)
        down_copies.append(
            pltpu.make_async_copy(pieces[i].at[pl.ds(start, rows)], sd.at[pl.ds(at, rows)], sem.at[i])
        )
    for c in up_copies + down_copies:
        c.start()
    for t in range(2):
        n_ref[t] = nt_ref[t].T
    for c in up_copies:
        c.wait()

    def columns(k):
        return pl.ds(pl.multiple_of(place_ref[k] * BLK, BLK), BLK)

    def slot(k):
        return pl.ds(pl.multiple_of(k * BLK, BLK), BLK)

    @pl.loop(0, 8)
    def _(k):
        pre = dot(n_ref[0], su[:, columns(k)]) * width_scale
        pre_ref[:, slot(k)] = pre
        act_ref[0, :, slot(k)] = gelu(pre).astype(bf16)

    for c in down_copies:
        c.wait()
    outs = [
        pltpu.make_async_copy(su.at[pl.ds(0, SEND)], send_ref, out_sem.at[0]),
        pltpu.make_async_copy(su.at[pl.ds(SEND, KEEP)], keep_ref, out_sem.at[1]),
        pltpu.make_async_copy(sd.at[pl.ds(0, EARLY)], early_ref, out_sem.at[2]),
        pltpu.make_async_copy(sd.at[pl.ds(EARLY, LATE)], late_ref, out_sem.at[3]),
    ]
    for c in outs:
        c.start()

    def grad_out(t, weight):
        @pl.loop(0, D // BLK)
        def _(j):
            outval = dot(act_ref[t], weight[:, slot(j)]) * hidden_scale
            resid = x_ref[t, :, slot(j)].astype(f32) + outval - t_ref[t, :, slot(j)].astype(f32)
            g_ref[t, :, slot(j)] = (resid * (1.0 / TOK)).astype(bf16)

    def grad_pre(t, weight):
        @pl.loop(0, 8)
        def _(k):
            grad_act = dot(g_ref[t], weight[slot(k), :], ((1,), (1,))) * hidden_scale
            gp_ref[t, :, columns(k)] = (grad_act * gelu_slope(pre_ref[:, slot(k)])).astype(bf16)

    grad_out(0, sd)
    grad_pre(0, sd)

    @pl.loop(0, 8)
    def _(k):
        raw = dot(nt_ref[0], gp_ref[0, :, columns(k)])
        w1u[...] = first_weight(su[:, columns(k)], raw, width_scale).astype(bf16)
        raw = dot(act_ref[0, :, slot(k)], g_ref[0], ((0,), (0,)))
        w1d[slot(k), :] = first_weight(sd[slot(k), :], raw, hidden_scale).astype(bf16)
        pre = dot(n_ref[1], w1u[...]) * width_scale
        pre_ref[:, slot(k)] = pre
        act_ref[1, :, slot(k)] = gelu(pre).astype(bf16)

    grad_out(1, w1d)
    grad_pre(1, w1d)
    for c in outs:
        c.wait()


def inner_steps(place, normed_t, x, t, up_pieces, down_pieces):
    vmem, hbm = pl.BlockSpec(memory_space=pltpu.VMEM), pl.BlockSpec(memory_space=pl.ANY)
    far = pl.BlockSpec(memory_space=pltpu.HBM)
    pieces = [p[0] for p in up_pieces + down_pieces]

    def kernel(*refs):
        inner_kernel([p[1:] for p in up_pieces], [p[1:] for p in down_pieces], *refs)

    return pl.pallas_call(
        kernel,
        out_shape=(
            jax.ShapeDtypeStruct((2, TOK, FFW), bf16),
            jax.ShapeDtypeStruct((2, TOK, D), bf16),
            jax.ShapeDtypeStruct((2, TOK, FFW), bf16),
            jax.ShapeDtypeStruct((SEND, FFW), bf16),
            jax.ShapeDtypeStruct((KEEP, FFW), bf16),
            jax.ShapeDtypeStruct((EARLY, D), bf16),
            jax.ShapeDtypeStruct((LATE, D), bf16),
        ),
        in_specs=[pl.BlockSpec(memory_space=pltpu.SMEM)] + [vmem] * 3 + [far] * len(pieces),
        out_specs=(vmem, vmem, vmem, hbm, hbm, hbm, hbm),
        scratch_shapes=[
            pltpu.VMEM((D, FFW), bf16),
            pltpu.VMEM((FFW, D), bf16),
            pltpu.VMEM((D, BLK), bf16),
            pltpu.VMEM((FFW, D), bf16),
            pltpu.VMEM((TOK, FFW), f32),
            pltpu.VMEM((2, TOK, D), bf16),
            pltpu.SemaphoreType.DMA((len(pieces),)),
            pltpu.SemaphoreType.DMA((4,)),
        ],
        compiler_params=pltpu.CompilerParams(vmem_limit_bytes=36 * 1024 * 1024),
        cost_estimate=pl.CostEstimate(flops=5 * 10**9, bytes_accessed=24 * 2**20, transcendentals=0),
        name="inner_steps",
    )(place, normed_t, x, t, *pieces)


def up_change(start, normed_t, grad_pre, first):
    rows = start.shape[0]
    wide = 2 * BLK

    def kernel(s_ref, n_ref, g_ref, o_ref):
        one = dot(n_ref[0, pl.ds(first, rows)], g_ref[0])
        two = dot(n_ref[1, pl.ds(first, rows)], g_ref[1])
        o_ref[...] = change_of(s_ref[...], one, two, width_scale)

    return pl.pallas_call(
        kernel,
        grid=(FFW // wide,),
        out_shape=jax.ShapeDtypeStruct((rows, FFW), bf16),
        in_specs=[
            pl.BlockSpec((rows, wide), lambda j: (0, j)),
            pl.BlockSpec((2, D, TOK), lambda j: (0, 0, 0)),
            pl.BlockSpec((2, TOK, wide), lambda j: (0, 0, j)),
        ],
        out_specs=pl.BlockSpec((rows, wide), lambda j: (0, j)),
        compiler_params=pltpu.CompilerParams(vmem_limit_bytes=24 * 1024 * 1024),
        cost_estimate=pl.CostEstimate(flops=4 * rows * TOK * FFW, bytes_accessed=4 * rows * FFW, transcendentals=0),
        name="up_change",
    )(start, normed_t, grad_pre)


def down_change(start, act, grad_out, first):
    rows = start.shape[0]

    def kernel(s_ref, a_ref, g_ref, *o_refs):
        one = dot(a_ref[0, :, pl.ds(first, rows)], g_ref[0], ((0,), (0,)))
        two = dot(a_ref[1, :, pl.ds(first, rows)], g_ref[1], ((0,), (0,)))
        change = change_of(s_ref[...], one, two, hidden_scale)
        for i, o_ref in enumerate(o_refs):
            o_ref[...] = change[BLK * i : BLK * i + BLK]

    return pl.pallas_call(
        kernel,
        grid=(D // BLK,),
        out_shape=(jax.ShapeDtypeStruct((BLK, D), bf16),) * (rows // BLK),
        in_specs=[
            pl.BlockSpec((rows, BLK), lambda j: (0, j)),
            pl.BlockSpec((2, TOK, FFW), lambda j: (0, 0, 0)),
            pl.BlockSpec((2, TOK, BLK), lambda j: (0, 0, j)),
        ],
        out_specs=(pl.BlockSpec((BLK, BLK), lambda j: (0, j)),) * (rows // BLK),
        compiler_params=pltpu.CompilerParams(vmem_limit_bytes=24 * 1024 * 1024),
        cost_estimate=pl.CostEstimate(flops=4 * rows * TOK * D, bytes_accessed=4 * rows * D, transcendentals=0),
        name="down_change",
    )(start, act, grad_out)


def local(inputs, targets, up_master, up_momentum, down_master, down_momentum):
    other, side, own = gather_up(up_master[0].astype(bf16))
    down_pieces = [
        (a, 0, BLK, BLK * i) for i, a in enumerate(gather_down(down_master[0].astype(bf16)))
    ]
    up_pieces, at = [], 0
    for a in other + side + own:
        up_pieces.append((a, 0, a.shape[0], at))
        at += a.shape[0]

    x, t = inputs[0, 0], targets[0, 0]
    feats = x.astype(f32)
    square_mean = jnp.mean(feats * feats, axis=-1, keepdims=True)
    normed = (feats * lax.rsqrt(square_mean + norm_eps)).astype(bf16)
    order = feature_order()
    rel_t = jnp.einsum("de,tnd->ten", order, normed, preferred_element_type=f32).astype(bf16)

    act, grad_out, grad_pre, up_other, up_keep, down_early, down_late = inner_steps(
        hidden_place(), rel_t, x, t, up_pieces, down_pieces
    )
    v_early = down_change(down_early, act, grad_out, 0)
    v_late = down_change(down_late, act, grad_out, EARLY)
    down_avg = scatter_down(*v_early, *v_late) / 8
    v_other = up_change(up_other, rel_t, grad_pre, 0)
    v_keep = up_change(up_keep, rel_t, grad_pre, SEND)
    up_avg = scatter_up(v_other, v_keep) / 32
    new_up_momentum = outer_beta * up_momentum + up_avg[None]
    new_up = up_master - outer_rate * (up_avg[None] + outer_beta * new_up_momentum)
    new_down_momentum = outer_beta * down_momentum + down_avg[None]
    new_down = down_master - outer_rate * (down_avg[None] + outer_beta * new_down_momentum)
    return (new_up, new_up_momentum, new_down, new_down_momentum)


def solution(mesh):
    in_specs = (
        P("row", "col", None, None, None),
        P("row", "col", None, None, None),
        P("col", "row", None),
        P("col", "row", None),
        P("row", "col", None),
        P("row", "col", None),
    )
    out_specs = (
        P("col", "row", None),
        P("col", "row", None),
        P("row", "col", None),
        P("row", "col", None),
    )
    return jax.shard_map(local, mesh=mesh, in_specs=in_specs, out_specs=out_specs, check_vma=False)
```

```python
import jax
import jax.numpy as jnp
from jax import lax
from jax.experimental import pallas as pl
from jax.experimental.pallas import tpu as pltpu
from jax.sharding import PartitionSpec as P

adam_rate = 0.05
beta_one = 0.9
beta_two = 0.95
adam_eps = 1e-06
decay_rate = 0.1
outer_rate = 0.7
outer_beta = 0.9
norm_eps = 1e-06

bf16 = jnp.bfloat16
f32 = jnp.float32

TOK, D, FFW = 128, 1024, 2048
BLK = 256
SEND, KEEP = 448, 576
EARLY, LATE = 768, 1280
width_scale = D ** (-0.5)
hidden_scale = FFW ** (-0.5)
ROOT = (2 / 3.141592653589793) ** 0.5


def swap_core(a):
    return lax.ppermute(a, "row", [(i, i ^ 1) for i in range(32)])


def swap_yh(a):
    return lax.ppermute(a, "row", [(i, i ^ 2) for i in range(32)])


def from_z(a):
    return lax.ppermute(a, "row", [(i, (i + (4 if i % 2 else -4)) % 32) for i in range(32)])


def to_z(a):
    return lax.ppermute(a, "row", [(i, (i + (-4 if i % 2 else 4)) % 32) for i in range(32)])


def swap_yl(a):
    return lax.ppermute(a, "col", [(i, i ^ 1) for i in range(8)])


def from_x(a, k):
    return lax.ppermute(a, "col", [(i, (i - 2 * k) % 8) for i in range(8)])


def up_order():
    own = [(0, 0, 0), (0, 1, 0), (0, 0, 1), (0, 1, 1)]
    side = [(k, y, c) for k in (1, 2, 3) for _, y, c in own] + [(4, 0, 0), (4, 1, 0)]
    other = [(-k, y, 1 - c) for k, y, c in side]
    return other, side, own


DOWN_ORDER = ((1, 1), (2, 1), (3, 1), (0, 1), (0, 0), (1, 0), (2, 0), (3, 0))


def after(a, *others):
    def kernel(*refs):
        pass

    anywhere = pl.BlockSpec(memory_space=pl.ANY)
    return pl.pallas_call(
        kernel,
        out_shape=jax.ShapeDtypeStruct(a.shape, a.dtype),
        in_specs=[anywhere] * (1 + len(others)),
        out_specs=anywhere,
        input_output_aliases={0: 0},
        name="after",
    )(a, *others)


def gather(up, down):
    b, d0 = swap_yh(up), swap_yl(down)
    c2 = from_x(down, 2)
    own = [up, b, swap_core(up), swap_core(b)]
    one = from_z(jnp.concatenate(own, 0))
    one = after(one, c2, d0)
    c1, c3, d2 = from_x(down, 1), from_x(down, -1), swap_yl(c2)
    two = from_z(one)
    two = after(two, c1, c3, d2)
    d1, d3 = from_x(d0, 1), from_x(d0, -1)
    three = from_z(two)
    side = [one, two, three, from_z(three[:64])]
    return [swap_core(s) for s in side], side, own, [d1, d2, d3, d0, down, c1, c2, c3]


def add(*parts):
    total = parts[0].astype(f32)
    for p in parts[1:]:
        total = total + p.astype(f32)
    return total


def scatter(v_other, v_keep, v_early, v_late):
    u1, u2, u3 = v_early
    u0, t0, t1, t2, t3 = v_late
    got = swap_core(v_other)

    def side(at, rows, *more):
        return add(v_keep[at : at + rows], got[at : at + rows], *more).astype(bf16)

    def wide(p):
        return jnp.pad(p, ((0, 64), (0, 0)))

    r = to_z(side(384, 64))
    p, m, w = from_x(u1, -1), from_x(u3, 1), swap_yl(u2)
    r = after(r, u1)
    r = to_z(side(256, 128, wide(r)))
    r = after(r, p, m, w, t0)
    r = to_z(side(128, 128, r))
    u0 = add(u0, p, m).astype(bf16)
    t2 = add(t2, w).astype(bf16)
    p, m = from_x(t1, -1), from_x(t3, 1)
    r = after(r, p, m)
    down = add(t0, p, m, from_x(t2, -2), swap_yl(u0))
    r = to_z(side(0, 128, r))
    away = add(v_keep[SEND + 64 :], r[64:]).astype(bf16)
    mine = add(v_keep[SEND : SEND + 64], r[:64], swap_core(away))
    up = mine[:32] + swap_yh(mine[32:].astype(bf16)).astype(f32)
    return up, down


def hidden_place():
    col = lax.axis_index("col")
    x, yl = col // 2, col % 2
    return jnp.stack([((x + dx) % 4) * 2 + (yl + dyl) % 2 for dx, dyl in DOWN_ORDER]).astype(jnp.int32)


def feature_order():
    row = lax.axis_index("row")
    z, yh, core = row // 4, (row // 2) % 2, row % 2
    sign = 1 - 2 * core
    other, side, own = up_order()
    first = jnp.stack(
        [((z + sign * k) % 8) * 4 + ((yh + y) % 2) * 2 + (core + c) % 2 for k, y, c in other + side + own]
    )
    place = (first[:, None] * 32 + jnp.arange(32)[None]).reshape(1, D)
    return (lax.broadcasted_iota(jnp.int32, (D, D), 0) == place).astype(bf16)


def dot(a, b, dims=((1,), (0,))):
    return lax.dot_general(a, b, (dims, ((), ())), preferred_element_type=f32)


def gelu(x):
    return 0.5 * x * (1.0 + jnp.tanh(ROOT * (x + 0.044715 * x * x * x)))


def gelu_slope(x):
    t = jnp.tanh(ROOT * (x + 0.044715 * x * x * x))
    return 0.5 * (1.0 + t) + 0.5 * x * (1.0 - t * t) * (ROOT * (1.0 + 3 * 0.044715 * x * x))


def first_weight(start, raw, scale):
    part = raw / (jnp.abs(raw) + adam_eps / scale)
    return (1 - adam_rate * decay_rate) * start.astype(f32) - adam_rate * part


def change_of(start, one, two, scale):
    eps = adam_eps / scale
    left = 1 - adam_rate * decay_rate
    ca, cb = (1 - beta_one) * beta_one / (1 - beta_one**2), (1 - beta_one) / (1 - beta_one**2)
    cc, cd = (1 - beta_two) * beta_two / (1 - beta_two**2), (1 - beta_two) / (1 - beta_two**2)
    part_one = one / ((jnp.abs(one) + eps) * (1 / (adam_rate * left)))
    square = one * one + (cd / cc) * (two * two)
    size = square * lax.rsqrt(jnp.maximum(square, 1e-36))
    root = cc**0.5
    part_two = (one + (cb / ca) * two) / ((size + eps / root) * (root / (adam_rate * ca)))
    return (part_one + part_two + (1 - left * left) * start.astype(f32)).astype(bf16)


def inner_kernel(up_pieces, down_pieces, *refs):
    count = len(up_pieces) + len(down_pieces)
    place_ref, nt_ref, x_ref, t_ref = refs[:4]
    pieces = refs[4 : 4 + count]
    act_ref, g_ref, gp_ref, send_ref, keep_ref, early_ref, late_ref = refs[4 + count : 11 + count]
    su, sd, w1u, w1d, pre_ref, n_ref, sem, out_sem = refs[11 + count :]

    up_copies, down_copies = [], []
    for i, (start, rows, at) in enumerate(up_pieces):
        up_copies.append(
            pltpu.make_async_copy(pieces[i].at[pl.ds(start, rows)], su.at[pl.ds(at, rows)], sem.at[i])
        )
    for j, (start, rows, at) in enumerate(down_pieces):
        i = j + len(up_pieces)
        down_copies.append(
            pltpu.make_async_copy(pieces[i].at[pl.ds(start, rows)], sd.at[pl.ds(at, rows)], sem.at[i])
        )
    for c in up_copies + down_copies:
        c.start()
    for t in range(2):
        n_ref[t] = nt_ref[t].T
    for c in up_copies:
        c.wait()

    def columns(k):
        return pl.ds(pl.multiple_of(place_ref[k] * BLK, BLK), BLK)

    def slot(k):
        return pl.ds(pl.multiple_of(k * BLK, BLK), BLK)

    @pl.loop(0, 8)
    def _(k):
        pre = dot(n_ref[0], su[:, columns(k)]) * width_scale
        pre_ref[:, slot(k)] = pre
        act_ref[0, :, slot(k)] = gelu(pre).astype(bf16)

    for c in down_copies:
        c.wait()
    outs = [
        pltpu.make_async_copy(su.at[pl.ds(0, SEND)], send_ref, out_sem.at[0]),
        pltpu.make_async_copy(su.at[pl.ds(SEND, KEEP)], keep_ref, out_sem.at[1]),
        pltpu.make_async_copy(sd.at[pl.ds(0, EARLY)], early_ref, out_sem.at[2]),
        pltpu.make_async_copy(sd.at[pl.ds(EARLY, LATE)], late_ref, out_sem.at[3]),
    ]
    for c in outs:
        c.start()

    def grad_out(t, weight):
        @pl.loop(0, D // BLK)
        def _(j):
            outval = dot(act_ref[t], weight[:, slot(j)]) * hidden_scale
            resid = x_ref[t, :, slot(j)].astype(f32) + outval - t_ref[t, :, slot(j)].astype(f32)
            g_ref[t, :, slot(j)] = (resid * (1.0 / TOK)).astype(bf16)

    def grad_pre(t, weight):
        @pl.loop(0, 8)
        def _(k):
            grad_act = dot(g_ref[t], weight[slot(k), :], ((1,), (1,))) * hidden_scale
            gp_ref[t, :, columns(k)] = (grad_act * gelu_slope(pre_ref[:, slot(k)])).astype(bf16)

    grad_out(0, sd)
    grad_pre(0, sd)

    @pl.loop(0, 8)
    def _(k):
        raw = dot(nt_ref[0], gp_ref[0, :, columns(k)])
        w1u[...] = first_weight(su[:, columns(k)], raw, width_scale).astype(bf16)
        raw = dot(act_ref[0, :, slot(k)], g_ref[0], ((0,), (0,)))
        w1d[slot(k), :] = first_weight(sd[slot(k), :], raw, hidden_scale).astype(bf16)
        pre = dot(n_ref[1], w1u[...]) * width_scale
        pre_ref[:, slot(k)] = pre
        act_ref[1, :, slot(k)] = gelu(pre).astype(bf16)

    grad_out(1, w1d)
    grad_pre(1, w1d)
    for c in outs:
        c.wait()


def inner_steps(place, normed_t, x, t, up_pieces, down_pieces):
    vmem, hbm = pl.BlockSpec(memory_space=pltpu.VMEM), pl.BlockSpec(memory_space=pl.ANY)
    far = pl.BlockSpec(memory_space=pltpu.HBM)
    pieces = [p[0] for p in up_pieces + down_pieces]

    def kernel(*refs):
        inner_kernel([p[1:] for p in up_pieces], [p[1:] for p in down_pieces], *refs)

    return pl.pallas_call(
        kernel,
        out_shape=(
            jax.ShapeDtypeStruct((2, TOK, FFW), bf16),
            jax.ShapeDtypeStruct((2, TOK, D), bf16),
            jax.ShapeDtypeStruct((2, TOK, FFW), bf16),
            jax.ShapeDtypeStruct((SEND, FFW), bf16),
            jax.ShapeDtypeStruct((KEEP, FFW), bf16),
            jax.ShapeDtypeStruct((EARLY, D), bf16),
            jax.ShapeDtypeStruct((LATE, D), bf16),
        ),
        in_specs=[pl.BlockSpec(memory_space=pltpu.SMEM)] + [vmem] * 3 + [far] * len(pieces),
        out_specs=(vmem, vmem, vmem, hbm, hbm, hbm, hbm),
        scratch_shapes=[
            pltpu.VMEM((D, FFW), bf16),
            pltpu.VMEM((FFW, D), bf16),
            pltpu.VMEM((D, BLK), bf16),
            pltpu.VMEM((FFW, D), bf16),
            pltpu.VMEM((TOK, FFW), f32),
            pltpu.VMEM((2, TOK, D), bf16),
            pltpu.SemaphoreType.DMA((len(pieces),)),
            pltpu.SemaphoreType.DMA((4,)),
        ],
        compiler_params=pltpu.CompilerParams(vmem_limit_bytes=36 * 1024 * 1024),
        cost_estimate=pl.CostEstimate(flops=5 * 10**9, bytes_accessed=24 * 2**20, transcendentals=0),
        name="inner_steps",
    )(place, normed_t, x, t, *pieces)


def up_change(start, normed_t, grad_pre, first):
    rows = start.shape[0]
    wide = 2 * BLK

    def kernel(s_ref, n_ref, g_ref, o_ref):
        one = dot(n_ref[0, pl.ds(first, rows)], g_ref[0])
        two = dot(n_ref[1, pl.ds(first, rows)], g_ref[1])
        o_ref[...] = change_of(s_ref[...], one, two, width_scale)

    return pl.pallas_call(
        kernel,
        grid=(FFW // wide,),
        out_shape=jax.ShapeDtypeStruct((rows, FFW), bf16),
        in_specs=[
            pl.BlockSpec((rows, wide), lambda j: (0, j)),
            pl.BlockSpec((2, D, TOK), lambda j: (0, 0, 0)),
            pl.BlockSpec((2, TOK, wide), lambda j: (0, 0, j)),
        ],
        out_specs=pl.BlockSpec((rows, wide), lambda j: (0, j)),
        compiler_params=pltpu.CompilerParams(vmem_limit_bytes=24 * 1024 * 1024),
        cost_estimate=pl.CostEstimate(flops=4 * rows * TOK * FFW, bytes_accessed=4 * rows * FFW, transcendentals=0),
        name="up_change",
    )(start, normed_t, grad_pre)


def down_change(start, act, grad_out, first):
    rows = start.shape[0]

    def kernel(s_ref, a_ref, g_ref, *o_refs):
        one = dot(a_ref[0, :, pl.ds(first, rows)], g_ref[0], ((0,), (0,)))
        two = dot(a_ref[1, :, pl.ds(first, rows)], g_ref[1], ((0,), (0,)))
        change = change_of(s_ref[...], one, two, hidden_scale)
        for i, o_ref in enumerate(o_refs):
            o_ref[...] = change[BLK * i : BLK * i + BLK]

    return pl.pallas_call(
        kernel,
        grid=(D // BLK,),
        out_shape=(jax.ShapeDtypeStruct((BLK, D), bf16),) * (rows // BLK),
        in_specs=[
            pl.BlockSpec((rows, BLK), lambda j: (0, j)),
            pl.BlockSpec((2, TOK, FFW), lambda j: (0, 0, 0)),
            pl.BlockSpec((2, TOK, BLK), lambda j: (0, 0, j)),
        ],
        out_specs=(pl.BlockSpec((BLK, BLK), lambda j: (0, j)),) * (rows // BLK),
        compiler_params=pltpu.CompilerParams(vmem_limit_bytes=24 * 1024 * 1024),
        cost_estimate=pl.CostEstimate(flops=4 * rows * TOK * D, bytes_accessed=4 * rows * D, transcendentals=0),
        name="down_change",
    )(start, act, grad_out)


def local(inputs, targets, up_master, up_momentum, down_master, down_momentum):
    other, side, own, down_blocks = gather(up_master[0].astype(bf16), down_master[0].astype(bf16))
    down_pieces = [(a, 0, BLK, BLK * i) for i, a in enumerate(down_blocks)]
    up_pieces, at = [], 0
    for a in other + side + own:
        up_pieces.append((a, 0, a.shape[0], at))
        at += a.shape[0]

    x, t = inputs[0, 0], targets[0, 0]
    feats = x.astype(f32)
    square_mean = jnp.mean(feats * feats, axis=-1, keepdims=True)
    normed = (feats * lax.rsqrt(square_mean + norm_eps)).astype(bf16)
    order = feature_order()
    rel_t = jnp.einsum("de,tnd->ten", order, normed, preferred_element_type=f32).astype(bf16)

    act, grad_out, grad_pre, up_other, up_keep, down_early, down_late = inner_steps(
        hidden_place(), rel_t, x, t, up_pieces, down_pieces
    )
    up_sum, down_sum = scatter(
        up_change(up_other, rel_t, grad_pre, 0),
        up_change(up_keep, rel_t, grad_pre, SEND),
        down_change(down_early, act, grad_out, 0),
        down_change(down_late, act, grad_out, EARLY),
    )
    up_avg, down_avg = up_sum / 32, down_sum / 8
    new_up_momentum = outer_beta * up_momentum + up_avg[None]
    new_up = up_master - outer_rate * (up_avg[None] + outer_beta * new_up_momentum)
    new_down_momentum = outer_beta * down_momentum + down_avg[None]
    new_down = down_master - outer_rate * (down_avg[None] + outer_beta * new_down_momentum)
    return (new_up, new_up_momentum, new_down, new_down_momentum)


def solution(mesh):
    in_specs = (
        P("row", "col", None, None, None),
        P("row", "col", None, None, None),
        P("col", "row", None),
        P("col", "row", None),
        P("row", "col", None),
        P("row", "col", None),
    )
    out_specs = (
        P("col", "row", None),
        P("col", "row", None),
        P("row", "col", None),
        P("row", "col", None),
    )
    return jax.shard_map(local, mesh=mesh, in_specs=in_specs, out_specs=out_specs, check_vma=False)
```

```python
import jax
import jax.numpy as jnp
from jax import lax
from jax.experimental import pallas as pl
from jax.experimental.pallas import tpu as pltpu
from jax.sharding import PartitionSpec as P

adam_rate = 0.05
beta_one = 0.9
beta_two = 0.95
adam_eps = 1e-06
decay_rate = 0.1
outer_rate = 0.7
outer_beta = 0.9
norm_eps = 1e-06

bf16 = jnp.bfloat16
f32 = jnp.float32

TOK, D, FFW = 128, 1024, 2048
BLK = 256
SEND, KEEP = 448, 576
EARLY, LATE = 768, 1280
width_scale = D ** (-0.5)
hidden_scale = FFW ** (-0.5)
ROOT = (2 / 3.141592653589793) ** 0.5


def swap_core(a):
    return lax.ppermute(a, "row", [(i, i ^ 1) for i in range(32)])


def swap_yh(a):
    return lax.ppermute(a, "row", [(i, i ^ 2) for i in range(32)])


def swap_both(a):
    return lax.ppermute(a, "row", [(i, i ^ 3) for i in range(32)])


def from_z(a):
    return lax.ppermute(a, "row", [(i, (i + (4 if i % 2 else -4)) % 32) for i in range(32)])


def to_z(a):
    return lax.ppermute(a, "row", [(i, (i + (-4 if i % 2 else 4)) % 32) for i in range(32)])


def swap_yl(a):
    return lax.ppermute(a, "col", [(i, i ^ 1) for i in range(8)])


def from_x(a, k):
    return lax.ppermute(a, "col", [(i, (i - 2 * k) % 8) for i in range(8)])


def up_order():
    own = [(0, 0, 0), (0, 1, 0), (0, 0, 1), (0, 1, 1)]
    side = [(k, y, c) for k in (1, 2, 3) for _, y, c in own] + [(4, 0, 0), (4, 1, 0)]
    other = [(-k, y, 1 - c) for k, y, c in side]
    return other, side, own


DOWN_ORDER = ((1, 1), (2, 1), (3, 1), (0, 1), (0, 0), (1, 0), (2, 0), (3, 0))


def after(*others):
    total = others[0][:1, :1]
    for o in others[1:]:
        total = total + o[:1, :1]
    return 0 * total


def hold(a, *others):
    return lax.dynamic_update_slice(a, a[:16, :128] + after(*others), (0, 0))


def gather(up, down, normed_t):
    own = [up, swap_yh(up), swap_core(up), swap_both(up)]
    c1, c3, d0 = from_x(down, 1), from_x(down, -1), swap_yl(down)
    one = from_z(jnp.concatenate(own, 0))
    one = hold(one, c1, c3)
    c2a, c2b = from_x(c1[:128], 1), from_x(c3[128:], -1)
    d1, d3 = from_x(d0, 1), from_x(d0, -1)
    two = from_z(one)
    two = hold(two, c2a, c2b, d0, normed_t[0])
    d2 = swap_yl(jnp.concatenate([c2a, c2b], 0))
    three = from_z(two)
    side = [one, two, three, from_z(three[:64])]
    return [swap_core(s) for s in side], side, own, [d1, d2, d3, d0, down, c1, c2a, c2b, c3]


def add(*parts):
    total = parts[0].astype(f32)
    for p in parts[1:]:
        total = total + p.astype(f32)
    return total


def scatter(v_other, v_keep, v_early, v_late):
    u1, u2, u3 = v_early
    u0, t0, t1, t2, t3 = v_late
    got = swap_core(v_other)

    def side(at, rows, *more):
        return add(v_keep[at : at + rows], got[at : at + rows], *more).astype(bf16)

    def wide(p):
        return jnp.pad(p, ((0, 64), (0, 0)))

    r = to_z(side(384, 64))
    p, m, w = from_x(u1, -1), from_x(u3, 1), swap_yl(u2)
    r = to_z(side(256, 128, wide(r), after(u1)))
    u0 = add(u0, p, m).astype(bf16)
    t2 = add(t2, w).astype(bf16)
    r = to_z(side(128, 128, r, after(u0, t2)))
    p, m, w = from_x(t2[:128], -1), from_x(t2[128:], 1), swap_yl(u0)
    t1 = add(t1, jnp.pad(p, ((0, 128), (0, 0)))).astype(bf16)
    t3 = add(t3, jnp.pad(m, ((128, 0), (0, 0)))).astype(bf16)
    r = to_z(side(0, 128, r, after(t1, t3)))
    p, m = from_x(t1, -1), from_x(t3, 1)
    down = add(t0, w, p, m)
    last = [add(v_keep[at : at + 32], r[at - SEND : at - SEND + 32]) for at in range(SEND, SEND + 128, 32)]
    yh, core, both = [a.astype(bf16) for a in last[1:]]
    up = add(last[0], swap_yh(yh), swap_core(core), swap_both(both))
    return up, down


def hidden_place():
    col = lax.axis_index("col")
    x, yl = col // 2, col % 2
    return jnp.stack([((x + dx) % 4) * 2 + (yl + dyl) % 2 for dx, dyl in DOWN_ORDER]).astype(jnp.int32)


def feature_order():
    row = lax.axis_index("row")
    z, yh, core = row // 4, (row // 2) % 2, row % 2
    sign = 1 - 2 * core
    other, side, own = up_order()
    first = jnp.stack(
        [((z + sign * k) % 8) * 4 + ((yh + y) % 2) * 2 + (core + c) % 2 for k, y, c in other + side + own]
    )
    place = (first[:, None] * 32 + jnp.arange(32)[None]).reshape(1, D)
    return (lax.broadcasted_iota(jnp.int32, (D, D), 0) == place).astype(bf16)


def dot(a, b, dims=((1,), (0,))):
    return lax.dot_general(a, b, (dims, ((), ())), preferred_element_type=f32)


def gelu(x):
    return 0.5 * x * (1.0 + jnp.tanh(ROOT * (x + 0.044715 * x * x * x)))


def gelu_slope(x):
    t = jnp.tanh(ROOT * (x + 0.044715 * x * x * x))
    return 0.5 * (1.0 + t) + 0.5 * x * (1.0 - t * t) * (ROOT * (1.0 + 3 * 0.044715 * x * x))


def first_weight(start, raw, scale):
    part = raw / (jnp.abs(raw) + adam_eps / scale)
    return (1 - adam_rate * decay_rate) * start.astype(f32) - adam_rate * part


def change_of(start, one, two, scale):
    eps = adam_eps / scale
    left = 1 - adam_rate * decay_rate
    ca, cb = (1 - beta_one) * beta_one / (1 - beta_one**2), (1 - beta_one) / (1 - beta_one**2)
    cc, cd = (1 - beta_two) * beta_two / (1 - beta_two**2), (1 - beta_two) / (1 - beta_two**2)
    part_one = one / ((jnp.abs(one) + eps) * (1 / (adam_rate * left)))
    square = one * one + (cd / cc) * (two * two)
    size = square * lax.rsqrt(jnp.maximum(square, 1e-36))
    root = cc**0.5
    part_two = (one + (cb / ca) * two) / ((size + eps / root) * (root / (adam_rate * ca)))
    return (part_one + part_two + (1 - left * left) * start.astype(f32)).astype(bf16)


def inner_kernel(up_pieces, down_pieces, *refs):
    count = len(up_pieces) + len(down_pieces)
    place_ref, nt_ref, x_ref, t_ref = refs[:4]
    pieces = refs[4 : 4 + count]
    act_ref, g_ref, gp_ref, send_ref, keep_ref, early_ref, late_ref = refs[4 + count : 11 + count]
    su, sd, w1u, w1d, pre_ref, n_ref, sem, out_sem = refs[11 + count :]

    up_copies, down_copies = [], []
    for i, (start, rows, at) in enumerate(up_pieces):
        up_copies.append(
            pltpu.make_async_copy(pieces[i].at[pl.ds(start, rows)], su.at[pl.ds(at, rows)], sem.at[i])
        )
    for j, (start, rows, at) in enumerate(down_pieces):
        i = j + len(up_pieces)
        down_copies.append(
            pltpu.make_async_copy(pieces[i].at[pl.ds(start, rows)], sd.at[pl.ds(at, rows)], sem.at[i])
        )
    for c in up_copies + down_copies:
        c.start()
    for t in range(2):
        n_ref[t] = nt_ref[t].T
    for c in up_copies:
        c.wait()

    def columns(k):
        return pl.ds(pl.multiple_of(place_ref[k] * BLK, BLK), BLK)

    def slot(k):
        return pl.ds(pl.multiple_of(k * BLK, BLK), BLK)

    @pl.loop(0, 8)
    def _(k):
        pre = dot(n_ref[0], su[:, columns(k)]) * width_scale
        pre_ref[:, slot(k)] = pre
        act_ref[0, :, slot(k)] = gelu(pre).astype(bf16)

    for c in down_copies:
        c.wait()
    outs = [
        pltpu.make_async_copy(su.at[pl.ds(0, SEND)], send_ref, out_sem.at[0]),
        pltpu.make_async_copy(su.at[pl.ds(SEND, KEEP)], keep_ref, out_sem.at[1]),
        pltpu.make_async_copy(sd.at[pl.ds(0, EARLY)], early_ref, out_sem.at[2]),
        pltpu.make_async_copy(sd.at[pl.ds(EARLY, LATE)], late_ref, out_sem.at[3]),
    ]
    for c in outs:
        c.start()

    def grad_out(t, weight):
        @pl.loop(0, D // BLK)
        def _(j):
            outval = dot(act_ref[t], weight[:, slot(j)]) * hidden_scale
            resid = x_ref[t, :, slot(j)].astype(f32) + outval - t_ref[t, :, slot(j)].astype(f32)
            g_ref[t, :, slot(j)] = (resid * (1.0 / TOK)).astype(bf16)

    def grad_pre(t, weight):
        @pl.loop(0, 8)
        def _(k):
            grad_act = dot(g_ref[t], weight[slot(k), :], ((1,), (1,))) * hidden_scale
            gp_ref[t, :, columns(k)] = (grad_act * gelu_slope(pre_ref[:, slot(k)])).astype(bf16)

    grad_out(0, sd)
    grad_pre(0, sd)

    @pl.loop(0, 8)
    def _(k):
        raw = dot(nt_ref[0], gp_ref[0, :, columns(k)])
        w1u[...] = first_weight(su[:, columns(k)], raw, width_scale).astype(bf16)
        raw = dot(act_ref[0, :, slot(k)], g_ref[0], ((0,), (0,)))
        w1d[slot(k), :] = first_weight(sd[slot(k), :], raw, hidden_scale).astype(bf16)
        pre = dot(n_ref[1], w1u[...]) * width_scale
        pre_ref[:, slot(k)] = pre
        act_ref[1, :, slot(k)] = gelu(pre).astype(bf16)

    grad_out(1, w1d)
    grad_pre(1, w1d)
    for c in outs:
        c.wait()


def inner_steps(place, normed_t, x, t, up_pieces, down_pieces):
    vmem, hbm = pl.BlockSpec(memory_space=pltpu.VMEM), pl.BlockSpec(memory_space=pl.ANY)
    far = pl.BlockSpec(memory_space=pltpu.HBM)
    pieces = [p[0] for p in up_pieces + down_pieces]

    def kernel(*refs):
        inner_kernel([p[1:] for p in up_pieces], [p[1:] for p in down_pieces], *refs)

    return pl.pallas_call(
        kernel,
        out_shape=(
            jax.ShapeDtypeStruct((2, TOK, FFW), bf16),
            jax.ShapeDtypeStruct((2, TOK, D), bf16),
            jax.ShapeDtypeStruct((2, TOK, FFW), bf16),
            jax.ShapeDtypeStruct((SEND, FFW), bf16),
            jax.ShapeDtypeStruct((KEEP, FFW), bf16),
            jax.ShapeDtypeStruct((EARLY, D), bf16),
            jax.ShapeDtypeStruct((LATE, D), bf16),
        ),
        in_specs=[pl.BlockSpec(memory_space=pltpu.SMEM)] + [vmem] * 3 + [far] * len(pieces),
        out_specs=(vmem, vmem, vmem, hbm, hbm, hbm, hbm),
        scratch_shapes=[
            pltpu.VMEM((D, FFW), bf16),
            pltpu.VMEM((FFW, D), bf16),
            pltpu.VMEM((D, BLK), bf16),
            pltpu.VMEM((FFW, D), bf16),
            pltpu.VMEM((TOK, FFW), f32),
            pltpu.VMEM((2, TOK, D), bf16),
            pltpu.SemaphoreType.DMA((len(pieces),)),
            pltpu.SemaphoreType.DMA((4,)),
        ],
        compiler_params=pltpu.CompilerParams(vmem_limit_bytes=36 * 1024 * 1024),
        cost_estimate=pl.CostEstimate(flops=5 * 10**9, bytes_accessed=24 * 2**20, transcendentals=0),
        name="inner_steps",
    )(place, normed_t, x, t, *pieces)


def up_change(start, normed_t, grad_pre, first):
    rows = start.shape[0]
    wide = 2 * BLK

    def kernel(s_ref, n_ref, g_ref, o_ref):
        one = dot(n_ref[0, pl.ds(first, rows)], g_ref[0])
        two = dot(n_ref[1, pl.ds(first, rows)], g_ref[1])
        o_ref[...] = change_of(s_ref[...], one, two, width_scale)

    return pl.pallas_call(
        kernel,
        grid=(FFW // wide,),
        out_shape=jax.ShapeDtypeStruct((rows, FFW), bf16),
        in_specs=[
            pl.BlockSpec((rows, wide), lambda j: (0, j)),
            pl.BlockSpec((2, D, TOK), lambda j: (0, 0, 0)),
            pl.BlockSpec((2, TOK, wide), lambda j: (0, 0, j)),
        ],
        out_specs=pl.BlockSpec((rows, wide), lambda j: (0, j)),
        compiler_params=pltpu.CompilerParams(vmem_limit_bytes=24 * 1024 * 1024),
        cost_estimate=pl.CostEstimate(flops=4 * rows * TOK * FFW, bytes_accessed=4 * rows * FFW, transcendentals=0),
        name="up_change",
    )(start, normed_t, grad_pre)


def down_change(start, act, grad_out, first):
    rows = start.shape[0]

    def kernel(s_ref, a_ref, g_ref, *o_refs):
        one = dot(a_ref[0, :, pl.ds(first, rows)], g_ref[0], ((0,), (0,)))
        two = dot(a_ref[1, :, pl.ds(first, rows)], g_ref[1], ((0,), (0,)))
        change = change_of(s_ref[...], one, two, hidden_scale)
        for i, o_ref in enumerate(o_refs):
            o_ref[...] = change[BLK * i : BLK * i + BLK]

    return pl.pallas_call(
        kernel,
        grid=(D // BLK,),
        out_shape=(jax.ShapeDtypeStruct((BLK, D), bf16),) * (rows // BLK),
        in_specs=[
            pl.BlockSpec((rows, BLK), lambda j: (0, j)),
            pl.BlockSpec((2, TOK, FFW), lambda j: (0, 0, 0)),
            pl.BlockSpec((2, TOK, BLK), lambda j: (0, 0, j)),
        ],
        out_specs=(pl.BlockSpec((BLK, BLK), lambda j: (0, j)),) * (rows // BLK),
        compiler_params=pltpu.CompilerParams(vmem_limit_bytes=24 * 1024 * 1024),
        cost_estimate=pl.CostEstimate(flops=4 * rows * TOK * D, bytes_accessed=4 * rows * D, transcendentals=0),
        name="down_change",
    )(start, act, grad_out)


def local(inputs, targets, up_master, up_momentum, down_master, down_momentum):
    x, t = inputs[0, 0], targets[0, 0]
    feats = x.astype(f32)
    square_mean = jnp.mean(feats * feats, axis=-1, keepdims=True)
    normed = (feats * lax.rsqrt(square_mean + norm_eps)).astype(bf16)
    order = feature_order()
    rel_t = jnp.einsum("de,tnd->ten", order, normed, preferred_element_type=f32).astype(bf16)

    other, side, own, down_blocks = gather(
        up_master[0].astype(bf16), down_master[0].astype(bf16), rel_t
    )
    down_pieces, at = [], 0
    for a in down_blocks:
        down_pieces.append((a, 0, a.shape[0], at))
        at += a.shape[0]
    up_pieces, at = [], 0
    for a in other + side + own:
        up_pieces.append((a, 0, a.shape[0], at))
        at += a.shape[0]

    act, grad_out, grad_pre, up_other, up_keep, down_early, down_late = inner_steps(
        hidden_place(), rel_t, x, t, up_pieces, down_pieces
    )
    up_sum, down_sum = scatter(
        up_change(up_other, rel_t, grad_pre, 0),
        up_change(up_keep, rel_t, grad_pre, SEND),
        down_change(down_early, act, grad_out, 0),
        down_change(down_late, act, grad_out, EARLY),
    )
    up_avg, down_avg = up_sum / 32, down_sum / 8
    new_up_momentum = outer_beta * up_momentum + up_avg[None]
    new_up = up_master - outer_rate * (up_avg[None] + outer_beta * new_up_momentum)
    new_down_momentum = outer_beta * down_momentum + down_avg[None]
    new_down = down_master - outer_rate * (down_avg[None] + outer_beta * new_down_momentum)
    return (new_up, new_up_momentum, new_down, new_down_momentum)


def solution(mesh):
    in_specs = (
        P("row", "col", None, None, None),
        P("row", "col", None, None, None),
        P("col", "row", None),
        P("col", "row", None),
        P("row", "col", None),
        P("row", "col", None),
    )
    out_specs = (
        P("col", "row", None),
        P("col", "row", None),
        P("row", "col", None),
        P("row", "col", None),
    )
    return jax.shard_map(local, mesh=mesh, in_specs=in_specs, out_specs=out_specs, check_vma=False)
```

```python
import jax
import jax.numpy as jnp
from jax import lax
from jax.experimental import pallas as pl
from jax.experimental.pallas import tpu as pltpu
from jax.sharding import PartitionSpec as P

adam_rate = 0.05
beta_one = 0.9
beta_two = 0.95
adam_eps = 1e-06
decay_rate = 0.1
outer_rate = 0.7
outer_beta = 0.9
norm_eps = 1e-06

bf16 = jnp.bfloat16
f32 = jnp.float32

TOK, D, FFW = 128, 1024, 2048
BLK = 256
SEND, KEEP = 448, 576
EARLY, LATE = 768, 1280
width_scale = D ** (-0.5)
hidden_scale = FFW ** (-0.5)
ROOT = (2 / 3.141592653589793) ** 0.5


def swap_core(a):
    return lax.ppermute(a, "row", [(i, i ^ 1) for i in range(32)])


def swap_yh(a):
    return lax.ppermute(a, "row", [(i, i ^ 2) for i in range(32)])


def swap_both(a):
    return lax.ppermute(a, "row", [(i, i ^ 3) for i in range(32)])


def from_z(a):
    return lax.ppermute(a, "row", [(i, (i + (4 if i % 2 else -4)) % 32) for i in range(32)])


def to_z(a):
    return lax.ppermute(a, "row", [(i, (i + (-4 if i % 2 else 4)) % 32) for i in range(32)])


def swap_yl(a):
    return lax.ppermute(a, "col", [(i, i ^ 1) for i in range(8)])


def from_x(a, k):
    return lax.ppermute(a, "col", [(i, (i - 2 * k) % 8) for i in range(8)])


def up_order():
    own = [(0, 0, 0), (0, 1, 0), (0, 0, 1), (0, 1, 1)]
    side = [(k, y, c) for k in (1, 2, 3) for _, y, c in own] + [(4, 0, 0), (4, 1, 0)]
    other = [(-k, y, 1 - c) for k, y, c in side]
    return other, side, own


DOWN_ORDER = ((1, 1), (2, 1), (3, 1), (0, 1), (0, 0), (1, 0), (2, 0), (3, 0))


def after(*others):
    total = others[0][:16, :128]
    for o in others[1:]:
        total = total + o[:16, :128]
    return 0 * total


def hold(a, *others):
    return lax.dynamic_update_slice(a, a[:16, :128] + after(*others), (0, 0))


def gather(up, down):
    own = [up, swap_yh(up), swap_core(up), swap_both(up)]
    c1, c3, d0 = from_x(down, 1), from_x(down, -1), swap_yl(down)
    one = from_z(jnp.concatenate(own, 0))
    one = hold(one, c1, c3)
    c2a, c2b = from_x(c1[:128], 1), from_x(c3[128:], -1)
    d1, d3 = from_x(d0, 1), from_x(d0, -1)
    two = from_z(one)
    two = hold(two, c2a, c2b, d0)
    d2 = swap_yl(jnp.concatenate([c2a, c2b], 0))
    three = from_z(two)
    side = [one, two, three, from_z(three[:64])]
    return [swap_core(s) for s in side], side, own, [d1, d2, d3, d0, down, c1, c2a, c2b, c3]


def add(*parts):
    total = parts[0].astype(f32)
    for p in parts[1:]:
        total = total + p.astype(f32)
    return total


def scatter(v_other, v_keep, v_early, late_change):
    u1, u2, u3 = v_early
    got = swap_core(v_other)

    def side(at, rows, *more):
        return add(v_keep[at : at + rows], got[at : at + rows], *more).astype(bf16)

    def wide(p):
        return jnp.pad(p, ((0, 128 - p.shape[0]), (0, FFW - p.shape[1])))

    r = to_z(side(384, 64))
    u0, t0, t1, t2, t3 = late_change(r)
    p, m, w = from_x(u1, -1), from_x(u3, 1), swap_yl(u2)
    r = to_z(side(256, 128, wide(r), wide(after(u1))))
    u0 = add(u0, p, m).astype(bf16)
    t2 = add(t2, w).astype(bf16)
    r = to_z(side(128, 128, r, wide(after(u0, t2))))
    p, m, w = from_x(t2[:128], -1), from_x(t2[128:], 1), swap_yl(u0)
    t1 = add(t1, jnp.pad(p, ((0, 128), (0, 0)))).astype(bf16)
    t3 = add(t3, jnp.pad(m, ((128, 0), (0, 0)))).astype(bf16)
    r = to_z(side(0, 128, r, wide(after(t1, t3))))
    p, m = from_x(t1, -1), from_x(t3, 1)
    down = add(t0, w, p, m)
    last = [add(v_keep[at : at + 32], r[at - SEND : at - SEND + 32]) for at in range(SEND, SEND + 128, 32)]
    yh, core, both = [a.astype(bf16) for a in last[1:]]
    up = add(last[0], swap_yh(yh), swap_core(core), swap_both(both))
    return up, down


def hidden_place(k):
    col = lax.axis_index("col")
    x, yl = col // 2, col % 2
    dx, dyl = DOWN_ORDER[k]
    return ((x + dx) % 4) * 2 + (yl + dyl) % 2


def feature_place():
    row = lax.axis_index("row")
    z, yh, core = row // 4, (row // 2) % 2, row % 2
    sign = 1 - 2 * core
    other, side, own = up_order()
    return [
        ((z + sign * k + 8) % 8) * 4 + ((yh + y) % 2) * 2 + (core + c) % 2 for k, y, c in other + side + own
    ]


def dot(a, b, dims=((1,), (0,))):
    return lax.dot_general(a, b, (dims, ((), ())), preferred_element_type=f32)


def gelu(x):
    return 0.5 * x * (1.0 + jnp.tanh(ROOT * (x + 0.044715 * x * x * x)))


def gelu_slope(x):
    t = jnp.tanh(ROOT * (x + 0.044715 * x * x * x))
    return 0.5 * (1.0 + t) + 0.5 * x * (1.0 - t * t) * (ROOT * (1.0 + 3 * 0.044715 * x * x))


def first_weight(start, raw, scale):
    part = raw / (jnp.abs(raw) + adam_eps / scale)
    return (1 - adam_rate * decay_rate) * start.astype(f32) - adam_rate * part


def change_of(start, one, two, scale):
    eps = adam_eps / scale
    left = 1 - adam_rate * decay_rate
    ca, cb = (1 - beta_one) * beta_one / (1 - beta_one**2), (1 - beta_one) / (1 - beta_one**2)
    cc, cd = (1 - beta_two) * beta_two / (1 - beta_two**2), (1 - beta_two) / (1 - beta_two**2)
    part_one = one / ((jnp.abs(one) + eps) * (1 / (adam_rate * left)))
    square = one * one + (cd / cc) * (two * two)
    size = square * lax.rsqrt(jnp.maximum(square, 1e-36))
    root = cc**0.5
    part_two = (one + (cb / ca) * two) / ((size + eps / root) * (root / (adam_rate * ca)))
    return (part_one + part_two + (1 - left * left) * start.astype(f32)).astype(bf16)


def prepare(x):
    def kernel(x_ref, n_ref, t_ref):
        lane = lax.broadcasted_iota(jnp.int32, (1, D), 1)
        place = lane
        for i, first in enumerate(feature_place()):
            place = jnp.where(lane // 32 == i, first * 32 + lane % 32, place)
        feats = x_ref[...].astype(f32)
        square_mean = jnp.mean(feats * feats, axis=-1, keepdims=True)
        normed = (feats * lax.rsqrt(square_mean + norm_eps)).astype(bf16).reshape(2 * TOK, D)
        for j in range(D // BLK):
            cols = slice(j * BLK, j * BLK + BLK)
            order = lax.broadcasted_iota(jnp.int32, (D, BLK), 0) == place[:, cols]
            part = dot(normed, order.astype(f32).astype(bf16))
            for t in range(2):
                rows = part[t * TOK : t * TOK + TOK]
                n_ref[t, :, cols] = rows.astype(bf16)
                t_ref[t, cols, :] = rows.T.astype(bf16)

    return pl.pallas_call(
        kernel,
        out_shape=(
            jax.ShapeDtypeStruct((2, TOK, D), bf16),
            jax.ShapeDtypeStruct((2, D, TOK), bf16),
        ),
        compiler_params=pltpu.CompilerParams(vmem_limit_bytes=12 * 1024 * 1024),
        cost_estimate=pl.CostEstimate(flops=2 * 10**8, bytes_accessed=2**21, transcendentals=0),
        name="prepare",
    )(x)


def inner_kernel(up_pieces, down_pieces, *refs):
    count = len(up_pieces) + len(down_pieces)
    n_ref, nt_ref, x_ref, t_ref = refs[:4]
    pieces = refs[4 : 4 + count]
    act_ref, g_ref, gp_ref, send_ref, keep_ref, early_ref, late_ref = refs[4 + count : 11 + count]
    su, sd, w1u, w1d, pre_ref, place_ref, sem, out_sem = refs[11 + count :]

    up_copies, down_copies = [], []
    for i, (start, rows, at) in enumerate(up_pieces):
        up_copies.append(
            pltpu.make_async_copy(pieces[i].at[pl.ds(start, rows)], su.at[pl.ds(at, rows)], sem.at[i])
        )
    for j, (start, rows, at) in enumerate(down_pieces):
        i = j + len(up_pieces)
        down_copies.append(
            pltpu.make_async_copy(pieces[i].at[pl.ds(start, rows)], sd.at[pl.ds(at, rows)], sem.at[i])
        )
    for c in up_copies + down_copies:
        c.start()
    for k in range(8):
        place_ref[k] = hidden_place(k)
    for c in up_copies:
        c.wait()

    def columns(k):
        return pl.ds(pl.multiple_of(place_ref[k] * BLK, BLK), BLK)

    def slot(k):
        return pl.ds(pl.multiple_of(k * BLK, BLK), BLK)

    @pl.loop(0, 8)
    def _(k):
        pre = dot(n_ref[0], su[:, columns(k)]) * width_scale
        pre_ref[:, slot(k)] = pre
        act_ref[0, :, slot(k)] = gelu(pre).astype(bf16)

    for c in down_copies:
        c.wait()
    outs = [
        pltpu.make_async_copy(su.at[pl.ds(0, SEND)], send_ref, out_sem.at[0]),
        pltpu.make_async_copy(su.at[pl.ds(SEND, KEEP)], keep_ref, out_sem.at[1]),
        pltpu.make_async_copy(sd.at[pl.ds(0, EARLY)], early_ref, out_sem.at[2]),
        pltpu.make_async_copy(sd.at[pl.ds(EARLY, LATE)], late_ref, out_sem.at[3]),
    ]
    for c in outs:
        c.start()

    def grad_out(t, weight):
        @pl.loop(0, D // BLK)
        def _(j):
            outval = dot(act_ref[t], weight[:, slot(j)]) * hidden_scale
            resid = x_ref[t, :, slot(j)].astype(f32) + outval - t_ref[t, :, slot(j)].astype(f32)
            g_ref[t, :, slot(j)] = (resid * (1.0 / TOK)).astype(bf16)

    def grad_pre(t, weight):
        @pl.loop(0, 8)
        def _(k):
            grad_act = dot(g_ref[t], weight[slot(k), :], ((1,), (1,))) * hidden_scale
            gp_ref[t, :, columns(k)] = (grad_act * gelu_slope(pre_ref[:, slot(k)])).astype(bf16)

    grad_out(0, sd)
    grad_pre(0, sd)

    @pl.loop(0, 8)
    def _(k):
        raw = dot(nt_ref[0], gp_ref[0, :, columns(k)])
        w1u[...] = first_weight(su[:, columns(k)], raw, width_scale).astype(bf16)
        raw = dot(act_ref[0, :, slot(k)], g_ref[0], ((0,), (0,)))
        w1d[slot(k), :] = first_weight(sd[slot(k), :], raw, hidden_scale).astype(bf16)
        pre = dot(n_ref[1], w1u[...]) * width_scale
        pre_ref[:, slot(k)] = pre
        act_ref[1, :, slot(k)] = gelu(pre).astype(bf16)

    grad_out(1, w1d)
    grad_pre(1, w1d)
    for c in outs:
        c.wait()


def inner_steps(normed, normed_t, x, t, up_pieces, down_pieces):
    vmem, hbm = pl.BlockSpec(memory_space=pltpu.VMEM), pl.BlockSpec(memory_space=pl.ANY)
    far = pl.BlockSpec(memory_space=pl.ANY)
    pieces = [p[0] for p in up_pieces + down_pieces]

    def kernel(*refs):
        inner_kernel([p[1:] for p in up_pieces], [p[1:] for p in down_pieces], *refs)

    return pl.pallas_call(
        kernel,
        out_shape=(
            jax.ShapeDtypeStruct((2, TOK, FFW), bf16),
            jax.ShapeDtypeStruct((2, TOK, D), bf16),
            jax.ShapeDtypeStruct((2, TOK, FFW), bf16),
            jax.ShapeDtypeStruct((SEND, FFW), bf16),
            jax.ShapeDtypeStruct((KEEP, FFW), bf16),
            jax.ShapeDtypeStruct((EARLY, D), bf16),
            jax.ShapeDtypeStruct((LATE, D), bf16),
        ),
        in_specs=[vmem] * 4 + [far] * len(pieces),
        out_specs=(vmem, vmem, vmem, hbm, hbm, hbm, hbm),
        scratch_shapes=[
            pltpu.VMEM((D, FFW), bf16),
            pltpu.VMEM((FFW, D), bf16),
            pltpu.VMEM((D, BLK), bf16),
            pltpu.VMEM((FFW, D), bf16),
            pltpu.VMEM((TOK, FFW), f32),
            pltpu.SMEM((8,), jnp.int32),
            pltpu.SemaphoreType.DMA((len(pieces),)),
            pltpu.SemaphoreType.DMA((4,)),
        ],
        compiler_params=pltpu.CompilerParams(vmem_limit_bytes=20 * 1024 * 1024),
        cost_estimate=pl.CostEstimate(flops=5 * 10**9, bytes_accessed=24 * 2**20, transcendentals=0),
        name="inner_steps",
    )(normed, normed_t, x, t, *pieces)


def up_change(start, normed_t, grad_pre, first):
    rows = start.shape[0]
    wide = 2 * BLK

    def kernel(s_ref, n_ref, g_ref, o_ref):
        one = dot(n_ref[0, pl.ds(first, rows)], g_ref[0])
        two = dot(n_ref[1, pl.ds(first, rows)], g_ref[1])
        o_ref[...] = change_of(s_ref[...], one, two, width_scale)

    return pl.pallas_call(
        kernel,
        grid=(FFW // wide,),
        out_shape=jax.ShapeDtypeStruct((rows, FFW), bf16),
        in_specs=[
            pl.BlockSpec((rows, wide), lambda j: (0, j)),
            pl.BlockSpec((2, D, TOK), lambda j: (0, 0, 0)),
            pl.BlockSpec((2, TOK, wide), lambda j: (0, 0, j)),
        ],
        out_specs=pl.BlockSpec((rows, wide), lambda j: (0, j)),
        compiler_params=pltpu.CompilerParams(vmem_limit_bytes=10 * 1024 * 1024),
        cost_estimate=pl.CostEstimate(flops=4 * rows * TOK * FFW, bytes_accessed=4 * rows * FFW, transcendentals=0),
        name="up_change",
    )(start, normed_t, grad_pre)


def down_change(start, act, grad_out, first, *awaited):
    rows = start.shape[0]

    def kernel(s_ref, a_ref, g_ref, *refs):
        o_refs = refs[len(awaited) :]
        one = dot(a_ref[0, :, pl.ds(first, rows)], g_ref[0], ((0,), (0,)))
        two = dot(a_ref[1, :, pl.ds(first, rows)], g_ref[1], ((0,), (0,)))
        change = change_of(s_ref[...], one, two, hidden_scale)
        for i, o_ref in enumerate(o_refs):
            o_ref[...] = change[BLK * i : BLK * i + BLK]

    return pl.pallas_call(
        kernel,
        grid=(D // BLK,),
        out_shape=(jax.ShapeDtypeStruct((BLK, D), bf16),) * (rows // BLK),
        in_specs=[
            pl.BlockSpec((rows, BLK), lambda j: (0, j)),
            pl.BlockSpec((2, TOK, FFW), lambda j: (0, 0, 0)),
            pl.BlockSpec((2, TOK, BLK), lambda j: (0, 0, j)),
        ]
        + [pl.BlockSpec(memory_space=pl.ANY)] * len(awaited),
        out_specs=(pl.BlockSpec((BLK, BLK), lambda j: (0, j)),) * (rows // BLK),
        compiler_params=pltpu.CompilerParams(vmem_limit_bytes=10 * 1024 * 1024),
        cost_estimate=pl.CostEstimate(flops=4 * rows * TOK * D, bytes_accessed=4 * rows * D, transcendentals=0),
        name="down_change",
    )(start, act, grad_out, *awaited)


def local(inputs, targets, up_master, up_momentum, down_master, down_momentum):
    x, t = inputs[0, 0], targets[0, 0]
    rel, rel_t = prepare(x)
    other, side, own, down_blocks = gather(
        up_master[0].astype(bf16), down_master[0].astype(bf16)
    )
    down_pieces, at = [], 0
    for a in down_blocks:
        down_pieces.append((a, 0, a.shape[0], at))
        at += a.shape[0]
    up_pieces, at = [], 0
    for a in other + side + own:
        up_pieces.append((a, 0, a.shape[0], at))
        at += a.shape[0]

    act, grad_out, grad_pre, up_other, up_keep, down_early, down_late = inner_steps(
        rel, rel_t, x, t, up_pieces, down_pieces
    )
    up_sum, down_sum = scatter(
        up_change(up_other, rel_t, grad_pre, 0),
        up_change(up_keep, rel_t, grad_pre, SEND),
        down_change(down_early, act, grad_out, 0),
        lambda r: down_change(down_late, act, grad_out, EARLY, r),
    )
    up_avg, down_avg = up_sum / 32, down_sum / 8
    new_up_momentum = outer_beta * up_momentum + up_avg[None]
    new_up = up_master - outer_rate * (up_avg[None] + outer_beta * new_up_momentum)
    new_down_momentum = outer_beta * down_momentum + down_avg[None]
    new_down = down_master - outer_rate * (down_avg[None] + outer_beta * new_down_momentum)
    return (new_up, new_up_momentum, new_down, new_down_momentum)


def solution(mesh):
    in_specs = (
        P("row", "col", None, None, None),
        P("row", "col", None, None, None),
        P("col", "row", None),
        P("col", "row", None),
        P("row", "col", None),
        P("row", "col", None),
    )
    out_specs = (
        P("col", "row", None),
        P("col", "row", None),
        P("row", "col", None),
        P("row", "col", None),
    )
    return jax.shard_map(local, mesh=mesh, in_specs=in_specs, out_specs=out_specs, check_vma=False)
```

```python
import jax
import jax.numpy as jnp
from jax import lax
from jax.experimental import pallas as pl
from jax.experimental.pallas import tpu as pltpu
from jax.sharding import PartitionSpec as P

adam_rate = 0.05
beta_one = 0.9
beta_two = 0.95
adam_eps = 1e-06
decay_rate = 0.1
outer_rate = 0.7
outer_beta = 0.9
norm_eps = 1e-06

bf16 = jnp.bfloat16
f32 = jnp.float32

TOK, D, FFW = 128, 1024, 2048
BLK = 256
SEND, KEEP = 448, 512
EARLY, LATE = 768, 1280
width_scale = D ** (-0.5)
hidden_scale = FFW ** (-0.5)
ROOT = (2 / 3.141592653589793) ** 0.5


def swap_core(a):
    return lax.ppermute(a, "row", [(i, i ^ 1) for i in range(32)])


def swap_yh(a):
    return lax.ppermute(a, "row", [(i, i ^ 2) for i in range(32)])


def swap_both(a):
    return lax.ppermute(a, "row", [(i, i ^ 3) for i in range(32)])


def from_z(a):
    return lax.ppermute(a, "row", [(i, (i + (4 if i % 2 else -4)) % 32) for i in range(32)])


def to_z(a):
    return lax.ppermute(a, "row", [(i, (i + (-4 if i % 2 else 4)) % 32) for i in range(32)])


def swap_yl(a):
    return lax.ppermute(a, "col", [(i, i ^ 1) for i in range(8)])


def from_x(a, k):
    return lax.ppermute(a, "col", [(i, (i - 2 * k) % 8) for i in range(8)])


def up_order():
    own = [(0, 0, 0), (0, 1, 0), (0, 0, 1), (0, 1, 1)]
    side = [(4, 0, 0), (4, 1, 0)] + [(k, y, c) for k in (1, 2, 3) for _, y, c in own]
    other = [(-k, y, 1 - c) for k, y, c in side]
    return other, side, own


DOWN_ORDER = ((1, 1), (2, 1), (3, 1), (0, 1), (0, 0), (1, 0), (2, 0), (3, 0))


def after(*others):
    total = others[0][:16, :128]
    for o in others[1:]:
        total = total + o[:16, :128]
    return 0 * total


def hold(a, *others):
    return lax.dynamic_update_slice(a, a[:16, :128] + after(*others), (0, 0))


def gather(up, down, normed_t):
    own = [up, swap_yh(up), swap_core(up), swap_both(up)]
    c1, c3, d0 = from_x(down, 1), from_x(down, -1), swap_yl(down)
    one = from_z(jnp.concatenate(own, 0))
    one = hold(one, c1, c3)
    c2a, c2b = from_x(c1[:128], 1), from_x(c3[128:], -1)
    d1, d3 = from_x(d0, 1), from_x(d0, -1)
    two = from_z(one)
    two = hold(two, c2a, c2b, d0, normed_t[0])
    d2 = swap_yl(jnp.concatenate([c2a, c2b], 0))
    three = from_z(two)
    side = [from_z(three[:64]), one, two, three]
    both = swap_core(jnp.concatenate(side[1:3], 0))
    other = [swap_core(side[0]), both, swap_core(side[3])]
    return other, side, own, [d1, d2, d3, d0, down, c1, c2a, c2b, c3]


def add(*parts):
    total = parts[0].astype(f32)
    for p in parts[1:]:
        total = total + p.astype(f32)
    return total


def scatter(v_first, v_keep, v_early, late_change):
    u1, u2, u3 = v_early
    v_other, v_four = v_first
    got = swap_core(v_other)

    def side(at, mine, *more):
        return add(mine, got[at : at + mine.shape[0]], *more).astype(bf16)

    def wide(p):
        return jnp.pad(p, ((0, 128 - p.shape[0]), (0, FFW - p.shape[1])))

    r = to_z(side(0, v_four))
    u0, t0, t1, t2, t3 = late_change(r)
    p, m, w = from_x(u1, -1), from_x(u3, 1), swap_yl(u2)
    r = to_z(side(320, v_keep[2], wide(r), wide(after(u1))))
    u0 = add(u0, p, m).astype(bf16)
    t2 = add(t2, w).astype(bf16)
    r = to_z(side(192, v_keep[1], r, wide(after(u0, t2))))
    p, m, w = from_x(t2[:128], -1), from_x(t2[128:], 1), swap_yl(u0)
    t1 = add(t1, jnp.pad(p, ((0, 128), (0, 0)))).astype(bf16)
    t3 = add(t3, jnp.pad(m, ((128, 0), (0, 0)))).astype(bf16)
    r = to_z(side(64, v_keep[0], r, wide(after(t1, t3))))
    p, m = from_x(t1, -1), from_x(t3, 1)
    down = add(t0, w, p, m)
    wait = jnp.pad(after(p, m, w), ((0, 48), (0, FFW - 128)))
    away = add(v_keep[4], r[64:], wait).astype(bf16)
    both = add(v_keep[3], r[:64], swap_core(away))
    up = both[:32] + swap_yh(both[32:].astype(bf16)).astype(f32)
    return up, down


def hidden_place(k):
    col = lax.axis_index("col")
    x, yl = col // 2, col % 2
    dx, dyl = DOWN_ORDER[k]
    return ((x + dx) % 4) * 2 + (yl + dyl) % 2


def feature_place():
    row = lax.axis_index("row")
    z, yh, core = row // 4, (row // 2) % 2, row % 2
    sign = 1 - 2 * core
    other, side, own = up_order()
    return [
        ((z + sign * k + 8) % 8) * 4 + ((yh + y) % 2) * 2 + (core + c) % 2 for k, y, c in other + side + own
    ]


def dot(a, b, dims=((1,), (0,))):
    return lax.dot_general(a, b, (dims, ((), ())), preferred_element_type=f32)


def gelu(x):
    return 0.5 * x * (1.0 + jnp.tanh(ROOT * (x + 0.044715 * x * x * x)))


def gelu_slope(x):
    t = jnp.tanh(ROOT * (x + 0.044715 * x * x * x))
    return 0.5 * (1.0 + t) + 0.5 * x * (1.0 - t * t) * (ROOT * (1.0 + 3 * 0.044715 * x * x))


def first_weight(start, raw, scale):
    part = raw / (jnp.abs(raw) + adam_eps / scale)
    return (1 - adam_rate * decay_rate) * start.astype(f32) - adam_rate * part


def change_of(start, one, two, scale):
    eps = adam_eps / scale
    left = 1 - adam_rate * decay_rate
    ca, cb = (1 - beta_one) * beta_one / (1 - beta_one**2), (1 - beta_one) / (1 - beta_one**2)
    cc, cd = (1 - beta_two) * beta_two / (1 - beta_two**2), (1 - beta_two) / (1 - beta_two**2)
    part_one = one / ((jnp.abs(one) + eps) * (1 / (adam_rate * left)))
    square = one * one + (cd / cc) * (two * two)
    size = square * lax.rsqrt(jnp.maximum(square, 1e-36))
    root = cc**0.5
    part_two = (one + (cb / ca) * two) / ((size + eps / root) * (root / (adam_rate * ca)))
    return (part_one + part_two + (1 - left * left) * start.astype(f32)).astype(bf16)


def prepare(x):
    def kernel(x_ref, n_ref, t_ref):
        lane = lax.broadcasted_iota(jnp.int32, (1, D), 1)
        place = lane
        for i, first in enumerate(feature_place()):
            place = jnp.where(lane // 32 == i, first * 32 + lane % 32, place)
        feats = x_ref[...].astype(f32)
        square_mean = jnp.mean(feats * feats, axis=-1, keepdims=True)
        normed = (feats * lax.rsqrt(square_mean + norm_eps)).astype(bf16).reshape(2 * TOK, D)
        for j in range(D // BLK):
            cols = slice(j * BLK, j * BLK + BLK)
            order = lax.broadcasted_iota(jnp.int32, (D, BLK), 0) == place[:, cols]
            part = dot(normed, order.astype(f32).astype(bf16))
            for t in range(2):
                rows = part[t * TOK : t * TOK + TOK]
                n_ref[t, :, cols] = rows.astype(bf16)
                t_ref[t, cols, :] = rows.T.astype(bf16)

    return pl.pallas_call(
        kernel,
        out_shape=(
            jax.ShapeDtypeStruct((2, TOK, D), bf16),
            jax.ShapeDtypeStruct((2, D, TOK), bf16),
        ),
        compiler_params=pltpu.CompilerParams(vmem_limit_bytes=12 * 1024 * 1024),
        cost_estimate=pl.CostEstimate(flops=2 * 10**8, bytes_accessed=2**21, transcendentals=0),
        name="prepare",
    )(x)


def inner_kernel(up_pieces, down_pieces, *refs):
    count = len(up_pieces) + len(down_pieces)
    n_ref, nt_ref, x_ref, t_ref = refs[:4]
    pieces = refs[4 : 4 + count]
    act_ref, g_ref, gp_ref, send_ref, keep_ref, early_ref, late_ref = refs[4 + count : 11 + count]
    su, sd, w1u, w1d, pre_ref, place_ref, sem, out_sem = refs[11 + count :]

    up_copies, down_copies = [], []
    for i, (start, rows, at) in enumerate(up_pieces):
        up_copies.append(
            pltpu.make_async_copy(pieces[i].at[pl.ds(start, rows)], su.at[pl.ds(at, rows)], sem.at[i])
        )
    for j, (start, rows, at) in enumerate(down_pieces):
        i = j + len(up_pieces)
        down_copies.append(
            pltpu.make_async_copy(pieces[i].at[pl.ds(start, rows)], sd.at[pl.ds(at, rows)], sem.at[i])
        )
    for c in up_copies + down_copies:
        c.start()
    for k in range(8):
        place_ref[k] = hidden_place(k)
    for c in up_copies:
        c.wait()

    def columns(k):
        return pl.ds(pl.multiple_of(place_ref[k] * BLK, BLK), BLK)

    def slot(k):
        return pl.ds(pl.multiple_of(k * BLK, BLK), BLK)

    @pl.loop(0, 8, unroll=True)
    def _(k):
        pre = dot(n_ref[0], su[:, columns(k)]) * width_scale
        pre_ref[:, slot(k)] = pre
        act_ref[0, :, slot(k)] = gelu(pre).astype(bf16)

    for c in down_copies:
        c.wait()
    outs = [
        pltpu.make_async_copy(su.at[pl.ds(0, D - KEEP)], send_ref, out_sem.at[0]),
        pltpu.make_async_copy(su.at[pl.ds(D - KEEP, KEEP)], keep_ref, out_sem.at[1]),
        pltpu.make_async_copy(sd.at[pl.ds(0, EARLY)], early_ref, out_sem.at[2]),
        pltpu.make_async_copy(sd.at[pl.ds(EARLY, LATE)], late_ref, out_sem.at[3]),
    ]
    for c in outs:
        c.start()

    def grad_out(t, weight):
        @pl.loop(0, D // BLK, unroll=True)
        def _(j):
            outval = dot(act_ref[t], weight[:, slot(j)]) * hidden_scale
            resid = x_ref[t, :, slot(j)].astype(f32) + outval - t_ref[t, :, slot(j)].astype(f32)
            g_ref[t, :, slot(j)] = (resid * (1.0 / TOK)).astype(bf16)

    def grad_pre(t, weight):
        @pl.loop(0, 8, unroll=True)
        def _(k):
            grad_act = dot(g_ref[t], weight[slot(k), :], ((1,), (1,))) * hidden_scale
            gp_ref[t, :, columns(k)] = (grad_act * gelu_slope(pre_ref[:, slot(k)])).astype(bf16)

    grad_out(0, sd)
    grad_pre(0, sd)

    @pl.loop(0, 8, unroll=4)
    def _(k):
        raw = dot(nt_ref[0], gp_ref[0, :, columns(k)])
        w1u[...] = first_weight(su[:, columns(k)], raw, width_scale).astype(bf16)
        raw = dot(act_ref[0, :, slot(k)], g_ref[0], ((0,), (0,)))
        w1d[slot(k), :] = first_weight(sd[slot(k), :], raw, hidden_scale).astype(bf16)
        pre = dot(n_ref[1], w1u[...]) * width_scale
        pre_ref[:, slot(k)] = pre
        act_ref[1, :, slot(k)] = gelu(pre).astype(bf16)

    grad_out(1, w1d)
    grad_pre(1, w1d)
    for c in outs:
        c.wait()


def inner_steps(normed, normed_t, x, t, up_pieces, down_pieces):
    vmem, hbm = pl.BlockSpec(memory_space=pltpu.VMEM), pl.BlockSpec(memory_space=pl.ANY)
    far = pl.BlockSpec(memory_space=pl.ANY)
    pieces = [p[0] for p in up_pieces + down_pieces]

    def kernel(*refs):
        inner_kernel([p[1:] for p in up_pieces], [p[1:] for p in down_pieces], *refs)

    return pl.pallas_call(
        kernel,
        out_shape=(
            jax.ShapeDtypeStruct((2, TOK, FFW), bf16),
            jax.ShapeDtypeStruct((2, TOK, D), bf16),
            jax.ShapeDtypeStruct((2, TOK, FFW), bf16),
            jax.ShapeDtypeStruct((D - KEEP, FFW), bf16),
            jax.ShapeDtypeStruct((KEEP, FFW), bf16),
            jax.ShapeDtypeStruct((EARLY, D), bf16),
            jax.ShapeDtypeStruct((LATE, D), bf16),
        ),
        in_specs=[vmem] * 4 + [far] * len(pieces),
        out_specs=(vmem, vmem, vmem, hbm, hbm, hbm, hbm),
        scratch_shapes=[
            pltpu.VMEM((D, FFW), bf16),
            pltpu.VMEM((FFW, D), bf16),
            pltpu.VMEM((D, BLK), bf16),
            pltpu.VMEM((FFW, D), bf16),
            pltpu.VMEM((TOK, FFW), f32),
            pltpu.SMEM((8,), jnp.int32),
            pltpu.SemaphoreType.DMA((len(pieces),)),
            pltpu.SemaphoreType.DMA((4,)),
        ],
        compiler_params=pltpu.CompilerParams(vmem_limit_bytes=24 * 1024 * 1024),
        cost_estimate=pl.CostEstimate(flops=5 * 10**9, bytes_accessed=24 * 2**20, transcendentals=0),
        name="inner_steps",
    )(normed, normed_t, x, t, *pieces)


def up_change(start, normed_t, grad_pre, first, parts):
    rows = start.shape[0]
    wide = 2 * BLK

    def kernel(s_ref, n_ref, g_ref, *o_refs):
        one = dot(n_ref[0, pl.ds(first, rows)], g_ref[0])
        two = dot(n_ref[1, pl.ds(first, rows)], g_ref[1])
        change = change_of(s_ref[...], one, two, width_scale)
        at = 0
        for part, o_ref in zip(parts, o_refs):
            o_ref[...] = change[at : at + part]
            at += part

    return pl.pallas_call(
        kernel,
        grid=(FFW // wide,),
        out_shape=tuple(jax.ShapeDtypeStruct((part, FFW), bf16) for part in parts),
        in_specs=[
            pl.BlockSpec((rows, wide), lambda j: (0, j)),
            pl.BlockSpec((2, D, TOK), lambda j: (0, 0, 0)),
            pl.BlockSpec((2, TOK, wide), lambda j: (0, 0, j)),
        ],
        out_specs=tuple(pl.BlockSpec((part, wide), lambda j: (0, j)) for part in parts),
        compiler_params=pltpu.CompilerParams(vmem_limit_bytes=10 * 1024 * 1024),
        cost_estimate=pl.CostEstimate(flops=4 * rows * TOK * FFW, bytes_accessed=4 * rows * FFW, transcendentals=0),
        name="up_change",
    )(start, normed_t, grad_pre)


def down_change(start, act, grad_out, first, *awaited):
    rows = start.shape[0]

    def kernel(s_ref, a_ref, g_ref, *refs):
        o_refs = refs[len(awaited) :]
        one = dot(a_ref[0, :, pl.ds(first, rows)], g_ref[0], ((0,), (0,)))
        two = dot(a_ref[1, :, pl.ds(first, rows)], g_ref[1], ((0,), (0,)))
        change = change_of(s_ref[...], one, two, hidden_scale)
        for i, o_ref in enumerate(o_refs):
            o_ref[...] = change[BLK * i : BLK * i + BLK]

    return pl.pallas_call(
        kernel,
        grid=(D // BLK,),
        out_shape=(jax.ShapeDtypeStruct((BLK, D), bf16),) * (rows // BLK),
        in_specs=[
            pl.BlockSpec((rows, BLK), lambda j: (0, j)),
            pl.BlockSpec((2, TOK, FFW), lambda j: (0, 0, 0)),
            pl.BlockSpec((2, TOK, BLK), lambda j: (0, 0, j)),
        ]
        + [pl.BlockSpec(memory_space=pl.ANY)] * len(awaited),
        out_specs=(pl.BlockSpec((BLK, BLK), lambda j: (0, j)),) * (rows // BLK),
        compiler_params=pltpu.CompilerParams(vmem_limit_bytes=10 * 1024 * 1024),
        cost_estimate=pl.CostEstimate(flops=4 * rows * TOK * D, bytes_accessed=4 * rows * D, transcendentals=0),
        name="down_change",
    )(start, act, grad_out, *awaited)


def local(inputs, targets, up_master, up_momentum, down_master, down_momentum):
    x, t = inputs[0, 0], targets[0, 0]
    rel, rel_t = prepare(x)
    other, side, own, down_blocks = gather(
        up_master[0].astype(bf16), down_master[0].astype(bf16), rel_t
    )
    down_pieces, at = [], 0
    for a in down_blocks:
        down_pieces.append((a, 0, a.shape[0], at))
        at += a.shape[0]
    up_pieces, at = [], 0
    for a in other + side + own:
        up_pieces.append((a, 0, a.shape[0], at))
        at += a.shape[0]

    act, grad_out, grad_pre, up_other, up_keep, down_early, down_late = inner_steps(
        rel, rel_t, x, t, up_pieces, down_pieces
    )
    up_sum, down_sum = scatter(
        up_change(up_other, rel_t, grad_pre, 0, (SEND, 64)),
        up_change(up_keep, rel_t, grad_pre, D - KEEP, (128, 128, 128, 64, 64)),
        down_change(down_early, act, grad_out, 0),
        lambda r: down_change(down_late, act, grad_out, EARLY, r),
    )
    up_avg, down_avg = up_sum / 32, down_sum / 8
    new_up_momentum = outer_beta * up_momentum + up_avg[None]
    new_up = up_master - outer_rate * (up_avg[None] + outer_beta * new_up_momentum)
    new_down_momentum = outer_beta * down_momentum + down_avg[None]
    new_down = down_master - outer_rate * (down_avg[None] + outer_beta * new_down_momentum)
    return (new_up, new_up_momentum, new_down, new_down_momentum)


def solution(mesh):
    in_specs = (
        P("row", "col", None, None, None),
        P("row", "col", None, None, None),
        P("col", "row", None),
        P("col", "row", None),
        P("row", "col", None),
        P("row", "col", None),
    )
    out_specs = (
        P("col", "row", None),
        P("col", "row", None),
        P("row", "col", None),
        P("row", "col", None),
    )
    return jax.shard_map(local, mesh=mesh, in_specs=in_specs, out_specs=out_specs, check_vma=False)
```

```python
import jax
import jax.numpy as jnp
from jax import lax
from jax.experimental import pallas as pl
from jax.experimental.pallas import tpu as pltpu
from jax.sharding import PartitionSpec as P

adam_rate = 0.05
beta_one = 0.9
beta_two = 0.95
adam_eps = 1e-06
decay_rate = 0.1
outer_rate = 0.7
outer_beta = 0.9
norm_eps = 1e-06

bf16 = jnp.bfloat16
f32 = jnp.float32

TOK, D, FFW = 128, 1024, 2048
BLK = 256
SEND, KEEP = 448, 512
EARLY, LATE = 768, 1280
width_scale = D ** (-0.5)
hidden_scale = FFW ** (-0.5)
ROOT = (2 / 3.141592653589793) ** 0.5


def swap_core(a):
    return lax.ppermute(a, "row", [(i, i ^ 1) for i in range(32)])


def swap_yh(a):
    return lax.ppermute(a, "row", [(i, i ^ 2) for i in range(32)])


def swap_both(a):
    return lax.ppermute(a, "row", [(i, i ^ 3) for i in range(32)])


def from_z(a):
    return lax.ppermute(a, "row", [(i, (i + (4 if i % 2 else -4)) % 32) for i in range(32)])


def to_z(a):
    return lax.ppermute(a, "row", [(i, (i + (-4 if i % 2 else 4)) % 32) for i in range(32)])


def swap_yl(a):
    return lax.ppermute(a, "col", [(i, i ^ 1) for i in range(8)])


def from_x(a, k):
    return lax.ppermute(a, "col", [(i, (i - 2 * k) % 8) for i in range(8)])


def up_order():
    own = [(0, 0, 0), (0, 1, 0), (0, 0, 1), (0, 1, 1)]
    side = [(4, 0, 0), (4, 1, 0)] + [(k, y, c) for k in (1, 2, 3) for _, y, c in own]
    other = [(-k, y, 1 - c) for k, y, c in side]
    return other, side, own


DOWN_ORDER = ((1, 1), (2, 1), (3, 1), (0, 1), (0, 0), (1, 0), (2, 0), (3, 0))


def after(*others):
    total = others[0][:16, :128]
    for o in others[1:]:
        total = total + o[:16, :128]
    return 0 * total


def hold(a, *others):
    return lax.dynamic_update_slice(a, a[:16, :128] + after(*others), (0, 0))


def gather(up, down, normed_t):
    own = [up, swap_yh(up), swap_core(up), swap_both(up)]
    c1, c3, d0 = from_x(down, 1), from_x(down, -1), swap_yl(down)
    one = from_z(jnp.concatenate(own, 0))
    one = hold(one, c1, c3)
    c2a, c2b = from_x(c1[:128], 1), from_x(c3[128:], -1)
    d1, d3 = from_x(d0, 1), from_x(d0, -1)
    two = from_z(one)
    two = hold(two, c2a, c2b, d0, normed_t[0])
    d2 = swap_yl(jnp.concatenate([c2a, c2b], 0))
    three = from_z(two)
    side = [from_z(three[:64]), one, two, three]
    both = swap_core(jnp.concatenate(side[1:3], 0))
    other = [swap_core(side[0]), both, swap_core(side[3])]
    return other, side, own, [d1, d2, d3, d0, down, c1, c2a, c2b, c3]


def add(*parts):
    total = parts[0].astype(f32)
    for p in parts[1:]:
        total = total + p.astype(f32)
    return total


def scatter(v_first, v_keep, v_early, late_change):
    u1, u2, u3 = v_early
    v_other, v_four = v_first
    got = swap_core(v_other)

    def side(at, mine, *more):
        return add(mine, got[at : at + mine.shape[0]], *more).astype(bf16)

    def wide(p):
        return jnp.pad(p, ((0, 128 - p.shape[0]), (0, FFW - p.shape[1])))

    r = to_z(side(0, v_four))
    u0, t0, t1, t2, t3 = late_change(r)
    p, m, w = from_x(u1, -1), from_x(u3, 1), swap_yl(u2)
    r = to_z(side(320, v_keep[2], wide(r), wide(after(u1))))
    u0 = add(u0, p, m).astype(bf16)
    t2 = add(t2, w).astype(bf16)
    r = to_z(side(192, v_keep[1], r, wide(after(u0, t2))))
    p, m, w = from_x(t2[:128], -1), from_x(t2[128:], 1), swap_yl(u0)
    t1 = add(t1, jnp.pad(p, ((0, 128), (0, 0)))).astype(bf16)
    t3 = add(t3, jnp.pad(m, ((128, 0), (0, 0)))).astype(bf16)
    r = to_z(side(64, v_keep[0], r, wide(after(t1, t3))))
    p, m = from_x(t1, -1), from_x(t3, 1)
    down = add(t0, w, p, m)
    wait = jnp.pad(after(p, m, w), ((0, 48), (0, FFW - 128)))
    away = add(v_keep[4], r[64:], wait).astype(bf16)
    both = add(v_keep[3], r[:64], swap_core(away))
    up = both[:32] + swap_yh(both[32:].astype(bf16)).astype(f32)
    return up, down


def hidden_place(k):
    col = lax.axis_index("col")
    x, yl = col // 2, col % 2
    dx, dyl = DOWN_ORDER[k]
    return ((x + dx) % 4) * 2 + (yl + dyl) % 2


def feature_place():
    row = lax.axis_index("row")
    z, yh, core = row // 4, (row // 2) % 2, row % 2
    sign = 1 - 2 * core
    other, side, own = up_order()
    return [
        ((z + sign * k + 8) % 8) * 4 + ((yh + y) % 2) * 2 + (core + c) % 2 for k, y, c in other + side + own
    ]


def dot(a, b, dims=((1,), (0,))):
    return lax.dot_general(a, b, (dims, ((), ())), preferred_element_type=f32)


def gelu(x):
    return 0.5 * x * (1.0 + jnp.tanh(ROOT * (x + 0.044715 * x * x * x)))


def gelu_slope(x):
    t = jnp.tanh(ROOT * (x + 0.044715 * x * x * x))
    return 0.5 * (1.0 + t) + 0.5 * x * (1.0 - t * t) * (ROOT * (1.0 + 3 * 0.044715 * x * x))


def first_weight(start, raw, scale):
    part = raw / (jnp.abs(raw) + adam_eps / scale)
    return (1 - adam_rate * decay_rate) * start.astype(f32) - adam_rate * part


def change_of(start, one, two, scale):
    eps = adam_eps / scale
    left = 1 - adam_rate * decay_rate
    ca, cb = (1 - beta_one) * beta_one / (1 - beta_one**2), (1 - beta_one) / (1 - beta_one**2)
    cc, cd = (1 - beta_two) * beta_two / (1 - beta_two**2), (1 - beta_two) / (1 - beta_two**2)
    part_one = one / ((jnp.abs(one) + eps) * (1 / (adam_rate * left)))
    square = one * one + (cd / cc) * (two * two)
    size = square * lax.rsqrt(jnp.maximum(square, 1e-36))
    root = cc**0.5
    part_two = (one + (cb / ca) * two) / ((size + eps / root) * (root / (adam_rate * ca)))
    return (part_one + part_two + (1 - left * left) * start.astype(f32)).astype(bf16)


def prepare(x):
    def kernel(x_ref, n_ref, t_ref):
        lane = lax.broadcasted_iota(jnp.int32, (1, D), 1)
        place = lane
        for i, first in enumerate(feature_place()):
            place = jnp.where(lane // 32 == i, first * 32 + lane % 32, place)
        feats = x_ref[...].astype(f32)
        square_mean = jnp.mean(feats * feats, axis=-1, keepdims=True)
        normed = (feats * lax.rsqrt(square_mean + norm_eps)).astype(bf16).reshape(2 * TOK, D)
        for j in range(D // BLK):
            cols = slice(j * BLK, j * BLK + BLK)
            order = lax.broadcasted_iota(jnp.int32, (D, BLK), 0) == place[:, cols]
            part = dot(normed, order.astype(f32).astype(bf16))
            for t in range(2):
                rows = part[t * TOK : t * TOK + TOK]
                n_ref[t, :, cols] = rows.astype(bf16)
                t_ref[t, cols, :] = rows.T.astype(bf16)

    return pl.pallas_call(
        kernel,
        out_shape=(
            jax.ShapeDtypeStruct((2, TOK, D), bf16),
            jax.ShapeDtypeStruct((2, D, TOK), bf16),
        ),
        compiler_params=pltpu.CompilerParams(vmem_limit_bytes=12 * 1024 * 1024),
        cost_estimate=pl.CostEstimate(flops=2 * 10**8, bytes_accessed=2**21, transcendentals=0),
        name="prepare",
    )(x)


def inner_kernel(up_pieces, down_pieces, *refs):
    count = len(up_pieces) + len(down_pieces)
    n_ref, nt_ref, x_ref, t_ref = refs[:4]
    pieces = refs[4 : 4 + count]
    act_ref, g_ref, gp_ref, send_ref, keep_ref, early_ref, late_ref = refs[4 + count : 11 + count]
    su, sd, w1u, w1d, pre_ref, place_ref, sem, out_sem = refs[11 + count :]

    up_copies, down_copies = [], []
    for i, (start, rows, at) in enumerate(up_pieces):
        up_copies.append(
            pltpu.make_async_copy(pieces[i].at[pl.ds(start, rows)], su.at[pl.ds(at, rows)], sem.at[i])
        )
    for j, (start, rows, at) in enumerate(down_pieces):
        i = j + len(up_pieces)
        down_copies.append(
            pltpu.make_async_copy(pieces[i].at[pl.ds(start, rows)], sd.at[pl.ds(at, rows)], sem.at[i])
        )
    for c in up_copies + down_copies:
        c.start()
    for k in range(8):
        place_ref[k] = hidden_place(k)
    for c in up_copies:
        c.wait()

    def columns(k):
        return pl.ds(pl.multiple_of(place_ref[k] * BLK, BLK), BLK)

    def slot(k):
        return pl.ds(pl.multiple_of(k * BLK, BLK), BLK)

    @pl.loop(0, 8, unroll=2)
    def _(k):
        pre = dot(n_ref[0], su[:, columns(k)]) * width_scale
        pre_ref[:, slot(k)] = pre
        act_ref[0, :, slot(k)] = gelu(pre).astype(bf16)

    for c in down_copies:
        c.wait()
    outs = [
        pltpu.make_async_copy(su.at[pl.ds(0, D - KEEP)], send_ref, out_sem.at[0]),
        pltpu.make_async_copy(su.at[pl.ds(D - KEEP, KEEP)], keep_ref, out_sem.at[1]),
        pltpu.make_async_copy(sd.at[pl.ds(0, EARLY)], early_ref, out_sem.at[2]),
        pltpu.make_async_copy(sd.at[pl.ds(EARLY, LATE)], late_ref, out_sem.at[3]),
    ]
    for c in outs:
        c.start()

    def grad_out(t, weight):
        @pl.loop(0, D // BLK, unroll=2)
        def _(j):
            outval = dot(act_ref[t], weight[:, slot(j)]) * hidden_scale
            resid = x_ref[t, :, slot(j)].astype(f32) + outval - t_ref[t, :, slot(j)].astype(f32)
            g_ref[t, :, slot(j)] = (resid * (1.0 / TOK)).astype(bf16)

    def grad_pre(t, weight):
        @pl.loop(0, 8, unroll=2)
        def _(k):
            grad_act = dot(g_ref[t], weight[slot(k), :], ((1,), (1,))) * hidden_scale
            gp_ref[t, :, columns(k)] = (grad_act * gelu_slope(pre_ref[:, slot(k)])).astype(bf16)

    grad_out(0, sd)
    grad_pre(0, sd)

    @pl.loop(0, 8, unroll=2)
    def _(k):
        raw = dot(nt_ref[0], gp_ref[0, :, columns(k)])
        w1u[...] = first_weight(su[:, columns(k)], raw, width_scale).astype(bf16)
        raw = dot(act_ref[0, :, slot(k)], g_ref[0], ((0,), (0,)))
        w1d[slot(k), :] = first_weight(sd[slot(k), :], raw, hidden_scale).astype(bf16)
        pre = dot(n_ref[1], w1u[...]) * width_scale
        pre_ref[:, slot(k)] = pre
        act_ref[1, :, slot(k)] = gelu(pre).astype(bf16)

    grad_out(1, w1d)
    grad_pre(1, w1d)
    for c in outs:
        c.wait()


def inner_steps(normed, normed_t, x, t, up_pieces, down_pieces):
    vmem, hbm = pl.BlockSpec(memory_space=pltpu.VMEM), pl.BlockSpec(memory_space=pl.ANY)
    far = pl.BlockSpec(memory_space=pl.ANY)
    pieces = [p[0] for p in up_pieces + down_pieces]

    def kernel(*refs):
        inner_kernel([p[1:] for p in up_pieces], [p[1:] for p in down_pieces], *refs)

    return pl.pallas_call(
        kernel,
        out_shape=(
            jax.ShapeDtypeStruct((2, TOK, FFW), bf16),
            jax.ShapeDtypeStruct((2, TOK, D), bf16),
            jax.ShapeDtypeStruct((2, TOK, FFW), bf16),
            jax.ShapeDtypeStruct((D - KEEP, FFW), bf16),
            jax.ShapeDtypeStruct((KEEP, FFW), bf16),
            jax.ShapeDtypeStruct((EARLY, D), bf16),
            jax.ShapeDtypeStruct((LATE, D), bf16),
        ),
        in_specs=[vmem] * 4 + [far] * len(pieces),
        out_specs=(vmem, vmem, vmem, hbm, hbm, hbm, hbm),
        scratch_shapes=[
            pltpu.VMEM((D, FFW), bf16),
            pltpu.VMEM((FFW, D), bf16),
            pltpu.VMEM((D, BLK), bf16),
            pltpu.VMEM((FFW, D), bf16),
            pltpu.VMEM((TOK, FFW), f32),
            pltpu.SMEM((8,), jnp.int32),
            pltpu.SemaphoreType.DMA((len(pieces),)),
            pltpu.SemaphoreType.DMA((4,)),
        ],
        compiler_params=pltpu.CompilerParams(vmem_limit_bytes=20 * 1024 * 1024),
        cost_estimate=pl.CostEstimate(flops=5 * 10**9, bytes_accessed=24 * 2**20, transcendentals=0),
        name="inner_steps",
    )(normed, normed_t, x, t, *pieces)


def up_change(start, normed_t, grad_pre, first, parts):
    rows = start.shape[0]
    wide = 2 * BLK

    def kernel(s_ref, n_ref, g_ref, *o_refs):
        one = dot(n_ref[0, pl.ds(first, rows)], g_ref[0])
        two = dot(n_ref[1, pl.ds(first, rows)], g_ref[1])
        change = change_of(s_ref[...], one, two, width_scale)
        at = 0
        for part, o_ref in zip(parts, o_refs):
            o_ref[...] = change[at : at + part]
            at += part

    return pl.pallas_call(
        kernel,
        grid=(FFW // wide,),
        out_shape=tuple(jax.ShapeDtypeStruct((part, FFW), bf16) for part in parts),
        in_specs=[
            pl.BlockSpec((rows, wide), lambda j: (0, j)),
            pl.BlockSpec((2, D, TOK), lambda j: (0, 0, 0)),
            pl.BlockSpec((2, TOK, wide), lambda j: (0, 0, j)),
        ],
        out_specs=tuple(pl.BlockSpec((part, wide), lambda j: (0, j)) for part in parts),
        compiler_params=pltpu.CompilerParams(vmem_limit_bytes=10 * 1024 * 1024),
        cost_estimate=pl.CostEstimate(flops=4 * rows * TOK * FFW, bytes_accessed=4 * rows * FFW, transcendentals=0),
        name="up_change",
    )(start, normed_t, grad_pre)


def down_change(start, act, grad_out, first, *awaited):
    rows = start.shape[0]

    def kernel(s_ref, a_ref, g_ref, *refs):
        o_refs = refs[len(awaited) :]
        one = dot(a_ref[0, :, pl.ds(first, rows)], g_ref[0], ((0,), (0,)))
        two = dot(a_ref[1, :, pl.ds(first, rows)], g_ref[1], ((0,), (0,)))
        change = change_of(s_ref[...], one, two, hidden_scale)
        for i, o_ref in enumerate(o_refs):
            o_ref[...] = change[BLK * i : BLK * i + BLK]

    return pl.pallas_call(
        kernel,
        grid=(D // BLK,),
        out_shape=(jax.ShapeDtypeStruct((BLK, D), bf16),) * (rows // BLK),
        in_specs=[
            pl.BlockSpec((rows, BLK), lambda j: (0, j)),
            pl.BlockSpec((2, TOK, FFW), lambda j: (0, 0, 0)),
            pl.BlockSpec((2, TOK, BLK), lambda j: (0, 0, j)),
        ]
        + [pl.BlockSpec(memory_space=pl.ANY)] * len(awaited),
        out_specs=(pl.BlockSpec((BLK, BLK), lambda j: (0, j)),) * (rows // BLK),
        compiler_params=pltpu.CompilerParams(vmem_limit_bytes=10 * 1024 * 1024),
        cost_estimate=pl.CostEstimate(flops=4 * rows * TOK * D, bytes_accessed=4 * rows * D, transcendentals=0),
        name="down_change",
    )(start, act, grad_out, *awaited)


def local(inputs, targets, up_master, up_momentum, down_master, down_momentum):
    x, t = inputs[0, 0], targets[0, 0]
    rel, rel_t = prepare(x)
    other, side, own, down_blocks = gather(
        up_master[0].astype(bf16), down_master[0].astype(bf16), rel_t
    )
    down_pieces, at = [], 0
    for a in down_blocks:
        down_pieces.append((a, 0, a.shape[0], at))
        at += a.shape[0]
    up_pieces, at = [], 0
    for a in other + side + own:
        up_pieces.append((a, 0, a.shape[0], at))
        at += a.shape[0]

    act, grad_out, grad_pre, up_other, up_keep, down_early, down_late = inner_steps(
        rel, rel_t, x, t, up_pieces, down_pieces
    )
    up_sum, down_sum = scatter(
        up_change(up_other, rel_t, grad_pre, 0, (SEND, 64)),
        up_change(up_keep, rel_t, grad_pre, D - KEEP, (128, 128, 128, 64, 64)),
        down_change(down_early, act, grad_out, 0),
        lambda r: down_change(down_late, act, grad_out, EARLY, r),
    )
    up_avg, down_avg = up_sum / 32, down_sum / 8
    new_up_momentum = outer_beta * up_momentum + up_avg[None]
    new_up = up_master - outer_rate * (up_avg[None] + outer_beta * new_up_momentum)
    new_down_momentum = outer_beta * down_momentum + down_avg[None]
    new_down = down_master - outer_rate * (down_avg[None] + outer_beta * new_down_momentum)
    return (new_up, new_up_momentum, new_down, new_down_momentum)


def solution(mesh):
    in_specs = (
        P("row", "col", None, None, None),
        P("row", "col", None, None, None),
        P("col", "row", None),
        P("col", "row", None),
        P("row", "col", None),
        P("row", "col", None),
    )
    out_specs = (
        P("col", "row", None),
        P("col", "row", None),
        P("row", "col", None),
        P("row", "col", None),
    )
    return jax.shard_map(local, mesh=mesh, in_specs=in_specs, out_specs=out_specs, check_vma=False)
```

```python
import jax
import jax.numpy as jnp
from jax import lax
from jax.experimental import pallas as pl
from jax.experimental.pallas import tpu as pltpu
from jax.sharding import PartitionSpec as P

adam_rate = 0.05
beta_one = 0.9
beta_two = 0.95
adam_eps = 1e-06
decay_rate = 0.1
outer_rate = 0.7
outer_beta = 0.9
norm_eps = 1e-06

bf16 = jnp.bfloat16
f32 = jnp.float32

TOK, D, FFW = 128, 1024, 2048
BLK = 256
SEND, KEEP = 448, 512
EARLY, LATE = 768, 1280
width_scale = D ** (-0.5)
hidden_scale = FFW ** (-0.5)
ROOT = (2 / 3.141592653589793) ** 0.5


def swap_core(a):
    return lax.ppermute(a, "row", [(i, i ^ 1) for i in range(32)])


def swap_yh(a):
    return lax.ppermute(a, "row", [(i, i ^ 2) for i in range(32)])


def swap_both(a):
    return lax.ppermute(a, "row", [(i, i ^ 3) for i in range(32)])


def from_z(a):
    return lax.ppermute(a, "row", [(i, (i + (4 if i % 2 else -4)) % 32) for i in range(32)])


def to_z(a):
    return lax.ppermute(a, "row", [(i, (i + (-4 if i % 2 else 4)) % 32) for i in range(32)])


def swap_yl(a):
    return lax.ppermute(a, "col", [(i, i ^ 1) for i in range(8)])


def from_x(a, k):
    return lax.ppermute(a, "col", [(i, (i - 2 * k) % 8) for i in range(8)])


def up_order():
    own = [(0, 0, 0), (0, 1, 0), (0, 0, 1), (0, 1, 1)]
    side = [(4, 0, 0), (4, 1, 0)] + [(k, y, c) for k in (1, 2, 3) for _, y, c in own]
    other = [(-k, y, 1 - c) for k, y, c in side]
    return other, side, own


DOWN_ORDER = ((1, 1), (2, 1), (3, 1), (0, 1), (0, 0), (1, 0), (2, 0), (3, 0))


def after(*others):
    total = others[0][:16, :128]
    for o in others[1:]:
        total = total + o[:16, :128]
    return 0 * total


def hold(a, *others):
    return lax.dynamic_update_slice(a, a[:16, :128] + after(*others), (0, 0))


def gather(up, down, normed_t):
    own = [up, swap_yh(up), swap_core(up), swap_both(up)]
    c1, c3, d0 = from_x(down, 1), from_x(down, -1), swap_yl(down)
    one = from_z(jnp.concatenate(own, 0))
    one = hold(one, c1, c3)
    c2a, c2b = from_x(c1[:128], 1), from_x(c3[128:], -1)
    d1, d3 = from_x(d0, 1), from_x(d0, -1)
    two = from_z(one)
    two = hold(two, c2a, c2b, d0, normed_t[0])
    d2 = swap_yl(jnp.concatenate([c2a, c2b], 0))
    three = from_z(two)
    side = [from_z(three[:64]), one, two, three]
    both = swap_core(jnp.concatenate(side[1:3], 0))
    other = [swap_core(side[0]), both, swap_core(side[3])]
    return other, side, own, [d1, d2, d3, d0, down, c1, c2a, c2b, c3]


def add(*parts):
    total = parts[0].astype(f32)
    for p in parts[1:]:
        total = total + p.astype(f32)
    return total


def scatter(v_first, v_keep, v_early, late_change):
    u1, u2, u3 = v_early
    v_other, v_four = v_first
    got = swap_core(v_other)

    def side(at, mine, *more):
        return add(mine, got[at : at + mine.shape[0]], *more).astype(bf16)

    def wide(p):
        return jnp.pad(p, ((0, 128 - p.shape[0]), (0, FFW - p.shape[1])))

    r = to_z(side(0, v_four))
    u0, t0, t1, t2, t3 = late_change(r)
    p, m, w = from_x(u1, -1), from_x(u3, 1), swap_yl(u2)
    r = to_z(side(320, v_keep[2], wide(r), wide(after(u1))))
    u0 = add(u0, p, m).astype(bf16)
    t2 = add(t2, w).astype(bf16)
    r = to_z(side(192, v_keep[1], r, wide(after(u0, t2))))
    p, m, w = from_x(t2[:128], -1), from_x(t2[128:], 1), swap_yl(u0)
    t1 = add(t1, jnp.pad(p, ((0, 128), (0, 0)))).astype(bf16)
    t3 = add(t3, jnp.pad(m, ((128, 0), (0, 0)))).astype(bf16)
    r = to_z(side(64, v_keep[0], r, wide(after(t1, t3))))
    p, m = from_x(t1, -1), from_x(t3, 1)
    down = add(t0, w, p, m)
    wait = jnp.pad(after(p, m, w), ((0, 48), (0, FFW - 128)))
    away = add(v_keep[4], r[64:], wait).astype(bf16)
    both = add(v_keep[3], r[:64], swap_core(away))
    up = both[:32] + swap_yh(both[32:].astype(bf16)).astype(f32)
    return up, down


def hidden_place(k):
    col = lax.axis_index("col")
    x, yl = col // 2, col % 2
    dx, dyl = DOWN_ORDER[k]
    return ((x + dx) % 4) * 2 + (yl + dyl) % 2


def feature_place():
    row = lax.axis_index("row")
    z, yh, core = row // 4, (row // 2) % 2, row % 2
    sign = 1 - 2 * core
    other, side, own = up_order()
    return [
        ((z + sign * k + 8) % 8) * 4 + ((yh + y) % 2) * 2 + (core + c) % 2 for k, y, c in other + side + own
    ]


def dot(a, b, dims=((1,), (0,))):
    return lax.dot_general(a, b, (dims, ((), ())), preferred_element_type=f32)


def gelu(x):
    return 0.5 * x * (1.0 + jnp.tanh(ROOT * (x + 0.044715 * x * x * x)))


def gelu_slope(x):
    t = jnp.tanh(ROOT * (x + 0.044715 * x * x * x))
    return 0.5 * (1.0 + t) + 0.5 * x * (1.0 - t * t) * (ROOT * (1.0 + 3 * 0.044715 * x * x))


def first_weight(start, raw, scale):
    part = raw / (jnp.abs(raw) + adam_eps / scale)
    return (1 - adam_rate * decay_rate) * start.astype(f32) - adam_rate * part


def change_of(start, one, two, scale):
    eps = adam_eps / scale
    left = 1 - adam_rate * decay_rate
    ca, cb = (1 - beta_one) * beta_one / (1 - beta_one**2), (1 - beta_one) / (1 - beta_one**2)
    cc, cd = (1 - beta_two) * beta_two / (1 - beta_two**2), (1 - beta_two) / (1 - beta_two**2)
    part_one = one / ((jnp.abs(one) + eps) * (1 / (adam_rate * left)))
    square = one * one + (cd / cc) * (two * two)
    size = square * lax.rsqrt(jnp.maximum(square, 1e-36))
    root = cc**0.5
    part_two = (one + (cb / ca) * two) / ((size + eps / root) * (root / (adam_rate * ca)))
    return (part_one + part_two + (1 - left * left) * start.astype(f32)).astype(bf16)


def prepare(x):
    def kernel(x_ref, n_ref, t_ref):
        lane = lax.broadcasted_iota(jnp.int32, (1, D), 1)
        place = lane
        for i, first in enumerate(feature_place()):
            place = jnp.where(lane // 32 == i, first * 32 + lane % 32, place)
        feats = x_ref[...].astype(f32)
        square_mean = jnp.mean(feats * feats, axis=-1, keepdims=True)
        normed = (feats * lax.rsqrt(square_mean + norm_eps)).astype(bf16).reshape(2 * TOK, D)
        for j in range(D // BLK):
            cols = slice(j * BLK, j * BLK + BLK)
            order = lax.broadcasted_iota(jnp.int32, (D, BLK), 0) == place[:, cols]
            part = dot(normed, order.astype(f32).astype(bf16))
            for t in range(2):
                rows = part[t * TOK : t * TOK + TOK]
                n_ref[t, :, cols] = rows.astype(bf16)
                t_ref[t, cols, :] = rows.T.astype(bf16)

    return pl.pallas_call(
        kernel,
        out_shape=(
            jax.ShapeDtypeStruct((2, TOK, D), bf16),
            jax.ShapeDtypeStruct((2, D, TOK), bf16),
        ),
        compiler_params=pltpu.CompilerParams(vmem_limit_bytes=12 * 1024 * 1024),
        cost_estimate=pl.CostEstimate(flops=2 * 10**8, bytes_accessed=2**21, transcendentals=0),
        name="prepare",
    )(x)


def inner_kernel(up_pieces, down_pieces, *refs):
    count = len(up_pieces) + len(down_pieces)
    n_ref, nt_ref, x_ref, t_ref = refs[:4]
    pieces = refs[4 : 4 + count]
    act_ref, g_ref, gp_ref, send_ref, keep_ref, early_ref, late_ref = refs[4 + count : 11 + count]
    su, sd, w1u, w1d, pre_ref, place_ref, sem, out_sem = refs[11 + count :]

    up_copies, down_copies = [], []
    for i, (start, rows, at) in enumerate(up_pieces):
        up_copies.append(
            pltpu.make_async_copy(pieces[i].at[pl.ds(start, rows)], su.at[pl.ds(at, rows)], sem.at[i])
        )
    for j, (start, rows, at) in enumerate(down_pieces):
        i = j + len(up_pieces)
        down_copies.append(
            pltpu.make_async_copy(pieces[i].at[pl.ds(start, rows)], sd.at[pl.ds(at, rows)], sem.at[i])
        )
    for c in up_copies + down_copies:
        c.start()
    for k in range(8):
        place_ref[k] = hidden_place(k)
    for c in up_copies:
        c.wait()

    def columns(k):
        return pl.ds(pl.multiple_of(place_ref[k] * BLK, BLK), BLK)

    def slot(k):
        return pl.ds(pl.multiple_of(k * BLK, BLK), BLK)

    @pl.loop(0, 8, unroll=2)
    def _(k):
        pre = dot(n_ref[0], su[:, columns(k)]) * width_scale
        pre_ref[:, slot(k)] = pre
        act_ref[0, :, slot(k)] = gelu(pre).astype(bf16)

    for c in down_copies:
        c.wait()
    outs = [
        pltpu.make_async_copy(su.at[pl.ds(0, D - KEEP)], send_ref, out_sem.at[0]),
        pltpu.make_async_copy(su.at[pl.ds(D - KEEP, KEEP)], keep_ref, out_sem.at[1]),
        pltpu.make_async_copy(sd.at[pl.ds(0, EARLY)], early_ref, out_sem.at[2]),
        pltpu.make_async_copy(sd.at[pl.ds(EARLY, LATE)], late_ref, out_sem.at[3]),
    ]
    for c in outs:
        c.start()

    def grad_out(t, weight):
        @pl.loop(0, D // BLK, unroll=2)
        def _(j):
            outval = dot(act_ref[t], weight[:, slot(j)]) * hidden_scale
            resid = x_ref[t, :, slot(j)].astype(f32) + outval - t_ref[t, :, slot(j)].astype(f32)
            g_ref[t, :, slot(j)] = (resid * (1.0 / TOK)).astype(bf16)

    def grad_pre(t, weight):
        @pl.loop(0, 8, unroll=2)
        def _(k):
            grad_act = dot(g_ref[t], weight[slot(k), :], ((1,), (1,))) * hidden_scale
            gp_ref[t, :, columns(k)] = (grad_act * gelu_slope(pre_ref[:, slot(k)])).astype(bf16)

    grad_out(0, sd)
    grad_pre(0, sd)

    @pl.loop(0, 8, unroll=4)
    def _(k):
        raw = dot(nt_ref[0], gp_ref[0, :, columns(k)])
        w1u[...] = first_weight(su[:, columns(k)], raw, width_scale).astype(bf16)
        raw = dot(act_ref[0, :, slot(k)], g_ref[0], ((0,), (0,)))
        w1d[slot(k), :] = first_weight(sd[slot(k), :], raw, hidden_scale).astype(bf16)
        pre = dot(n_ref[1], w1u[...]) * width_scale
        pre_ref[:, slot(k)] = pre
        act_ref[1, :, slot(k)] = gelu(pre).astype(bf16)

    grad_out(1, w1d)
    grad_pre(1, w1d)
    for c in outs:
        c.wait()


def inner_steps(normed, normed_t, x, t, up_pieces, down_pieces):
    vmem, hbm = pl.BlockSpec(memory_space=pltpu.VMEM), pl.BlockSpec(memory_space=pl.ANY)
    far = pl.BlockSpec(memory_space=pl.ANY)
    pieces = [p[0] for p in up_pieces + down_pieces]

    def kernel(*refs):
        inner_kernel([p[1:] for p in up_pieces], [p[1:] for p in down_pieces], *refs)

    return pl.pallas_call(
        kernel,
        out_shape=(
            jax.ShapeDtypeStruct((2, TOK, FFW), bf16),
            jax.ShapeDtypeStruct((2, TOK, D), bf16),
            jax.ShapeDtypeStruct((2, TOK, FFW), bf16),
            jax.ShapeDtypeStruct((D - KEEP, FFW), bf16),
            jax.ShapeDtypeStruct((KEEP, FFW), bf16),
            jax.ShapeDtypeStruct((EARLY, D), bf16),
            jax.ShapeDtypeStruct((LATE, D), bf16),
        ),
        in_specs=[vmem] * 4 + [far] * len(pieces),
        out_specs=(vmem, vmem, vmem, hbm, hbm, hbm, hbm),
        scratch_shapes=[
            pltpu.VMEM((D, FFW), bf16),
            pltpu.VMEM((FFW, D), bf16),
            pltpu.VMEM((D, BLK), bf16),
            pltpu.VMEM((FFW, D), bf16),
            pltpu.VMEM((TOK, FFW), f32),
            pltpu.SMEM((8,), jnp.int32),
            pltpu.SemaphoreType.DMA((len(pieces),)),
            pltpu.SemaphoreType.DMA((4,)),
        ],
        compiler_params=pltpu.CompilerParams(vmem_limit_bytes=20 * 1024 * 1024),
        cost_estimate=pl.CostEstimate(flops=5 * 10**9, bytes_accessed=24 * 2**20, transcendentals=0),
        name="inner_steps",
    )(normed, normed_t, x, t, *pieces)


def up_change(start, normed_t, grad_pre, first, parts):
    rows = start.shape[0]
    wide = 2 * BLK

    def kernel(s_ref, n_ref, g_ref, *o_refs):
        one = dot(n_ref[0, pl.ds(first, rows)], g_ref[0])
        two = dot(n_ref[1, pl.ds(first, rows)], g_ref[1])
        change = change_of(s_ref[...], one, two, width_scale)
        at = 0
        for part, o_ref in zip(parts, o_refs):
            o_ref[...] = change[at : at + part]
            at += part

    return pl.pallas_call(
        kernel,
        grid=(FFW // wide,),
        out_shape=tuple(jax.ShapeDtypeStruct((part, FFW), bf16) for part in parts),
        in_specs=[
            pl.BlockSpec((rows, wide), lambda j: (0, j)),
            pl.BlockSpec((2, D, TOK), lambda j: (0, 0, 0)),
            pl.BlockSpec((2, TOK, wide), lambda j: (0, 0, j)),
        ],
        out_specs=tuple(pl.BlockSpec((part, wide), lambda j: (0, j)) for part in parts),
        compiler_params=pltpu.CompilerParams(vmem_limit_bytes=10 * 1024 * 1024),
        cost_estimate=pl.CostEstimate(flops=4 * rows * TOK * FFW, bytes_accessed=4 * rows * FFW, transcendentals=0),
        name="up_change",
    )(start, normed_t, grad_pre)


def down_change(start, act, grad_out, first, *awaited):
    rows = start.shape[0]

    def kernel(s_ref, a_ref, g_ref, *refs):
        o_refs = refs[len(awaited) :]
        one = dot(a_ref[0, :, pl.ds(first, rows)], g_ref[0], ((0,), (0,)))
        two = dot(a_ref[1, :, pl.ds(first, rows)], g_ref[1], ((0,), (0,)))
        change = change_of(s_ref[...], one, two, hidden_scale)
        for i, o_ref in enumerate(o_refs):
            o_ref[...] = change[BLK * i : BLK * i + BLK]

    return pl.pallas_call(
        kernel,
        grid=(D // BLK,),
        out_shape=(jax.ShapeDtypeStruct((BLK, D), bf16),) * (rows // BLK),
        in_specs=[
            pl.BlockSpec((rows, BLK), lambda j: (0, j)),
            pl.BlockSpec((2, TOK, FFW), lambda j: (0, 0, 0)),
            pl.BlockSpec((2, TOK, BLK), lambda j: (0, 0, j)),
        ]
        + [pl.BlockSpec(memory_space=pl.ANY)] * len(awaited),
        out_specs=(pl.BlockSpec((BLK, BLK), lambda j: (0, j)),) * (rows // BLK),
        compiler_params=pltpu.CompilerParams(vmem_limit_bytes=10 * 1024 * 1024),
        cost_estimate=pl.CostEstimate(flops=4 * rows * TOK * D, bytes_accessed=4 * rows * D, transcendentals=0),
        name="down_change",
    )(start, act, grad_out, *awaited)


def local(inputs, targets, up_master, up_momentum, down_master, down_momentum):
    x, t = inputs[0, 0], targets[0, 0]
    rel, rel_t = prepare(x)
    other, side, own, down_blocks = gather(
        up_master[0].astype(bf16), down_master[0].astype(bf16), rel_t
    )
    down_pieces, at = [], 0
    for a in down_blocks:
        down_pieces.append((a, 0, a.shape[0], at))
        at += a.shape[0]
    up_pieces, at = [], 0
    for a in other + side + own:
        up_pieces.append((a, 0, a.shape[0], at))
        at += a.shape[0]

    act, grad_out, grad_pre, up_other, up_keep, down_early, down_late = inner_steps(
        rel, rel_t, x, t, up_pieces, down_pieces
    )
    up_sum, down_sum = scatter(
        up_change(up_other, rel_t, grad_pre, 0, (SEND, 64)),
        up_change(up_keep, rel_t, grad_pre, D - KEEP, (128, 128, 128, 64, 64)),
        down_change(down_early, act, grad_out, 0),
        lambda r: down_change(down_late, act, grad_out, EARLY, r),
    )
    up_avg, down_avg = up_sum / 32, down_sum / 8
    new_up_momentum = outer_beta * up_momentum + up_avg[None]
    new_up = up_master - outer_rate * (up_avg[None] + outer_beta * new_up_momentum)
    new_down_momentum = outer_beta * down_momentum + down_avg[None]
    new_down = down_master - outer_rate * (down_avg[None] + outer_beta * new_down_momentum)
    return (new_up, new_up_momentum, new_down, new_down_momentum)


def solution(mesh):
    in_specs = (
        P("row", "col", None, None, None),
        P("row", "col", None, None, None),
        P("col", "row", None),
        P("col", "row", None),
        P("row", "col", None),
        P("row", "col", None),
    )
    out_specs = (
        P("col", "row", None),
        P("col", "row", None),
        P("row", "col", None),
        P("row", "col", None),
    )
    return jax.shard_map(local, mesh=mesh, in_specs=in_specs, out_specs=out_specs, check_vma=False)
```
